256 devices in a mesh: row: 64 (over z, x, core), rep: 4 (over y).
Axes of the slice: x: 4, y: 4, z: 8, core: 2. Of those that a mesh axis runs over, the one named last changes fastest.
Arguments:
- features: bfloat16 [32768, 128], P(('row', 'rep')), may hold values from -6 to 6
- weight: bfloat16 [128, 128], replicated, may hold values from -0.5 to 0.5
- bias_terms: float32 [128], replicated, may hold values from -3 to 3
- cotangent: bfloat16 [32768, 128], P(('row', 'rep')), may hold values from -6 to 6
- tile_values: bfloat16 [64, 4, 128, 128, 128], P('row', 'rep'), may hold values from 0 to 0.026977539
- tile_rows: int32 [64, 4, 128], P('row', 'rep'), may hold values from 0 to 3, as said below
- tile_cols: int32 [64, 4, 128], P('row', 'rep'), may hold values from 0 to 63
- tile_count: int32 [64, 4], P('row', 'rep'), may hold values from 64 to 128, as said below
Outputs:
- output: bfloat16 [32768, 128], P(('row', 'rep'))
- grad_input: bfloat16 [32768, 128], P(('row', 'rep'))
- weight_grad: float32 [128, 128], replicated
- bias_grad: float32 [128], replicated
The draws below stay inside these ranges and needn't reach their ends.
Inputs may be any that keep to these rules, and one draw needn't show every extreme that they name: Within one device the pairs (tile_rows, tile_cols) of its 128 slots are distinct. `tile_count`: some device has all 128 slots live.
All inputs are finite; a program needn't handle non-finite values.
Results may differ from the reference program's by a relative error of at most 0.008.
Values may be sent and summed in bfloat16 or wider, within the bound.
No kernel may reach another device: no remote copies, remote signals or barrier semaphores. Data moves between devices by JAX's collectives and lax.ppermute only.
A program may use at most 64 MiB of HBM per device.

```python
import jax
import jax.numpy as jnp
from jax import lax

F = 128
HID = 128
TILE = 128
ROW_TILES = 1
PANEL_TILES = 4
COL_TILES = 64
SLOTS = 128
NODES = 32768
N_ROW = 64
N_REP = 4


def tile_positions(key):
    keylist = jax.random.split(key, N_ROW * N_REP)

    def single_device(subkey):
        return jax.random.permutation(subkey, PANEL_TILES * COL_TILES)[:SLOTS]
    positions = jax.vmap(single_device)(keylist)
    return positions.reshape(N_ROW, N_REP, SLOTS).astype(jnp.int32)


def draw_tile_rows(key, part):
    return tile_positions(key) // COL_TILES


def draw_tile_cols(key, part):
    return tile_positions(key) % COL_TILES


def draw_tile_count(key, part):
    key = jax.random.fold_in(key, 7)
    first_key, second_key = jax.random.split(key)
    fewest = max(SLOTS // 2, 1)
    counts = jax.random.randint(first_key, (N_ROW * N_REP,), fewest, SLOTS + 1)
    chosen = jax.random.randint(second_key, (), 0, N_ROW * N_REP)
    flattened = counts.at[chosen].set(SLOTS)
    flattened = flattened.at[(chosen + 1) % (N_ROW * N_REP)].set(fewest)
    return flattened.reshape(N_ROW, N_REP).astype(jnp.int32)


def block_levels(own_key, dims, cuts, low, high):
    loudness, own = 1.0, jax.random.fold_in(own_key, 6)
    for dim, blocks in cuts:
        heights = jnp.exp(jax.random.uniform(jax.random.fold_in(own, dim), (blocks,), jnp.float32, low / len(cuts), high / len(cuts)))
        loudness = loudness * jnp.repeat(heights, dims[dim] // blocks).reshape([-1 if axis == dim else 1 for axis in range(len(dims))])
    return loudness


def centred(stream_key, shape, spread, limit, shards=(), kind=jnp.bfloat16):
    drawn = spread * jax.random.normal(stream_key, shape, jnp.float32)
    if shards:
        drawn = drawn * block_levels(stream_key, shape, shards, -0.22, 0.18)
    return jnp.clip(drawn, -limit, limit).astype(kind)


def setup_inputs(seed: int = 0) -> dict:
    streams_of = jax.random.split(jax.random.key(seed), 9)
    return {
        "features": centred(streams_of[0], (NODES, F), 1.0, 6.0, ((0, 256),)),
        "weight": centred(streams_of[1], (F, HID), F ** -0.5, 0.5),
        "bias_terms": centred(streams_of[2], (HID,), 0.5, 3.0, (), jnp.float32),
        "cotangent": centred(streams_of[3], (NODES, HID), 1.0, 6.0, ((0, 256),)),
        "tile_values": jnp.clip(0.026977539 * jax.random.uniform(streams_of[4], (N_ROW, N_REP, SLOTS, TILE, TILE), jnp.float32) ** block_levels(streams_of[4], (N_ROW, N_REP, SLOTS, TILE, TILE), ((0, 64), (1, 4)), -0.2, 0.2), 0.0, 0.026977539).astype(jnp.bfloat16),
        "tile_rows": draw_tile_rows(jax.random.fold_in(streams_of[8], 71), 0),
        "tile_cols": draw_tile_cols(jax.random.fold_in(streams_of[8], 71), 0),
        "tile_count": draw_tile_count(jax.random.fold_in(streams_of[8], 71), 0),
    }


def reference(features, weight, bias_terms, cotangent, tile_values, tile_rows, tile_cols, tile_count):
    row_count = ROW_TILES * TILE
    panel_rows = N_REP * row_count
    by_part = features.reshape(N_ROW, N_REP, row_count, F)
    slot_ids = jnp.arange(SLOTS, dtype=jnp.int32)
    dev_ids = jnp.arange(N_ROW * N_REP, dtype=jnp.int32)

    def forward_one(dev_index):
        row_index = dev_index // N_REP
        rep_index = dev_index % N_REP
        column_blocks = by_part[:, rep_index].reshape(COL_TILES, TILE, F).astype(jnp.float32)
        tile_block = tile_values[row_index, rep_index].astype(jnp.float32)
        live_slots = (slot_ids < tile_count[row_index, rep_index]).astype(jnp.float32)
        picked = column_blocks[tile_cols[row_index, rep_index]]
        products = jnp.einsum('kij,kjf->kif', tile_block, picked) * live_slots[:, None, None]
        summed = jax.ops.segment_sum(products, tile_rows[row_index, rep_index], num_segments=PANEL_TILES)
        return summed.reshape(panel_rows, F)

    partials = lax.map(forward_one, dev_ids)
    aggregated = partials.reshape(N_ROW, N_REP, panel_rows, F).sum(axis=1).reshape(NODES, F).astype(jnp.bfloat16)
    preact = jnp.dot(aggregated, weight, preferred_element_type=jnp.float32) + bias_terms
    output = jax.nn.silu(preact).astype(jnp.bfloat16)
    sigmoid_pre = jax.nn.sigmoid(preact)
    grad_pre = (cotangent.astype(jnp.float32) * sigmoid_pre * (1.0 + preact * (1.0 - sigmoid_pre))).astype(jnp.bfloat16)
    grad_scale = NODES ** -0.5
    weight_grad = jnp.dot(aggregated.T, grad_pre, preferred_element_type=jnp.float32) * grad_scale
    bias_grad = jnp.sum(grad_pre.astype(jnp.float32), axis=0) * grad_scale
    back_rows = jnp.dot(grad_pre, weight.T, preferred_element_type=jnp.float32).astype(jnp.bfloat16)
    panels = back_rows.reshape(N_ROW, PANEL_TILES, TILE, F)

    def backward_one(carry, dev_index):
        row_index = dev_index // N_REP
        rep_index = dev_index % N_REP
        panel_blocks = panels[row_index].astype(jnp.float32)
        tile_block = tile_values[row_index, rep_index].astype(jnp.float32)
        live_slots = (slot_ids < tile_count[row_index, rep_index]).astype(jnp.float32)
        picked = panel_blocks[tile_rows[row_index, rep_index]]
        products = jnp.einsum('kji,kjf->kif', tile_block, picked) * live_slots[:, None, None]
        contrib = jax.ops.segment_sum(products, tile_cols[row_index, rep_index], num_segments=COL_TILES)
        return carry.at[rep_index].add(contrib), None

    start = jnp.zeros((N_REP, COL_TILES, TILE, F), jnp.float32)
    totals, unused = lax.scan(backward_one, start, dev_ids)
    grad_input = totals.reshape(N_REP, N_ROW, row_count, F).transpose(1, 0, 2, 3).reshape(NODES, F).astype(jnp.bfloat16)
    return output, grad_input, weight_grad, bias_grad
```

```python
import jax
import jax.numpy as jnp
from jax import lax
from jax.experimental import pallas as pl
from jax.experimental.pallas import tpu as pltpu
from jax.sharding import Mesh
from jax.sharding import PartitionSpec as P

Z, X, C, Q = 8, 4, 2, 4
T = 128
PANEL = Q * T
SLOTS = 128
HALF = T // 2
PAY = HALF + 16
MSG = Z * T + PAY
BLK = T + PAY
F32 = jnp.float32
BF16 = jnp.bfloat16
ROW = ("z", "x", "core")
ALL = ("z", "x", "core", "rep")
SCALE = (Z * X * C * Q * T) ** -0.5

VMEM = pl.BlockSpec(memory_space=pltpu.VMEM)
SMEM = pl.BlockSpec(memory_space=pltpu.SMEM)


def params(mib):
    return pltpu.CompilerParams(vmem_limit_bytes=mib * 2**20)


def shift(axis, size, by):
    return [(i, (i + by) % size) for i in range(size)]


def send(array, axis, size, by):
    return lax.ppermute(array, axis, shift(axis, size, by))


def densify_kernel(rows_ref, cols_ref, count_ref, me_ref, tiles_ref, dense_ref):
    def clear(p, carry):
        dense_ref[p] = jnp.zeros((PANEL, T), BF16)
        return carry

    lax.fori_loop(0, Z * X * C, clear, 0)
    x, core = me_ref[0], me_ref[1]

    def place(k, carry):
        col = cols_ref[k]
        z_col = col // (X * C)
        x_col = (col // C) % X
        core_col = col % C
        offset = (x - x_col + X) % X
        other = (core + core_col) % C
        position = (offset * C + other) * Z + z_col
        row = pl.multiple_of(rows_ref[k] * T, T)
        dense_ref[position, pl.ds(row, T), :] = tiles_ref[k]
        return carry

    lax.fori_loop(0, count_ref[0], place, 0)


def densify(rows, cols, count, me, tiles):
    return pl.pallas_call(
        densify_kernel,
        in_specs=[SMEM, SMEM, SMEM, SMEM, VMEM],
        out_specs=VMEM,
        out_shape=jax.ShapeDtypeStruct((Z * X * C, PANEL, T), BF16),
        compiler_params=params(16),
        name="densify",
    )(rows, cols, count, me, tiles)


def forward(dense, gathered):
    def kernel(dense_ref, *refs):
        sources, out_ref, total = refs[:-2], refs[-2], refs[-1]
        for n, source in enumerate(sources):
            panel = jnp.concatenate([dense_ref[n * Z + z] for z in range(Z)], axis=1)
            part = jnp.dot(panel, source[...].reshape(Z * T, T), preferred_element_type=F32)
            if n == 0:
                total[...] = part
            else:
                total[...] += part
        out_ref[...] = total[...].astype(BF16)

    return pl.pallas_call(
        kernel,
        in_specs=[VMEM] * (1 + len(gathered)),
        out_specs=VMEM,
        out_shape=jax.ShapeDtypeStruct((PANEL, T), BF16),
        scratch_shapes=[pltpu.VMEM((PANEL, T), F32)],
        compiler_params=params(16),
        name="forward",
    )(dense, *gathered)


def split(value):
    high = value.astype(BF16)
    low = (value - high.astype(F32)).astype(BF16)
    return high, low


def pack_bias(ref, start, value):
    high, low = split(value)
    rows = lax.broadcasted_iota(jnp.int32, (16, T), 0)
    packed = jnp.where(rows == 0, high.astype(F32), jnp.where(rows == 1, low.astype(F32), 0.0))
    ref[start:start + 16, :] = packed.astype(BF16)


def middle_kernel(me_ref, p0, p1, p2, p3, c0, c1, c2, c3, weight_ref, bias_ref,
                  out_ref, back_ref, keep_ref, pay_ref, cot, pre, wsum):
    rep, core = me_ref[2], me_ref[1]
    for n, source in enumerate((c0, c1, c2, c3)):
        cot[(rep - n + Q) % Q] = source[...]
    total = (p0[...].astype(F32) + p2[...].astype(F32)) + (p1[...].astype(F32) + p3[...].astype(F32))
    aggregated = total.astype(BF16)
    preact = jnp.dot(aggregated, weight_ref[...], preferred_element_type=F32) + bias_ref[...]
    pre[...] = preact.reshape(Q, T, T)
    sig = jax.nn.sigmoid(preact)
    cotangent = cot[...].reshape(PANEL, T).astype(F32)
    grad_pre = (cotangent * sig * (1.0 + preact * (1.0 - sig))).astype(BF16)
    own = pre[rep]
    out_ref[...] = (own * jax.nn.sigmoid(own)).astype(BF16)
    back = lax.dot_general(weight_ref[...], grad_pre, (((1,), (1,)), ((), ())), preferred_element_type=F32)
    back_ref[...] = back.astype(BF16)
    terms = lax.dot_general(aggregated, grad_pre, (((0,), (0,)), ((), ())), preferred_element_type=F32)
    wsum[...] = terms.reshape(C, HALF, T)
    bias_sum = jnp.sum(grad_pre.astype(F32), axis=0, keepdims=True)
    keep_ref[:HALF] = wsum[core]
    high, low = split(bias_sum)
    keep_ref[HALF:HALF + 1] = high.astype(F32) + low.astype(F32)
    keep_ref[HALF + 1:] = jnp.zeros((15, T), F32)
    pay_ref[:HALF] = wsum[1 - core].astype(BF16)
    pack_bias(pay_ref, HALF, bias_sum)


def middle(me, partials, cotangents, weight, bias):
    return pl.pallas_call(
        middle_kernel,
        in_specs=[SMEM] + [VMEM] * 10,
        out_specs=[VMEM] * 4,
        out_shape=[
            jax.ShapeDtypeStruct((T, T), BF16),
            jax.ShapeDtypeStruct((T, PANEL), BF16),
            jax.ShapeDtypeStruct((PAY, T), F32),
            jax.ShapeDtypeStruct((PAY, T), BF16),
        ],
        scratch_shapes=[
            pltpu.VMEM((Q, T, T), BF16),
            pltpu.VMEM((Q, T, T), F32),
            pltpu.VMEM((C, HALF, T), F32),
        ],
        compiler_params=params(16),
        name="middle",
    )(me, *partials, *cotangents, weight, bias)


def backward(dense, back, chunk):
    def kernel(dense_ref, back_ref, mine_ref, theirs_ref):
        for n, ref in enumerate((mine_ref, theirs_ref)):
            for z in range(0, Z, 2):
                at = (chunk * C + n) * Z + z
                pair = jnp.concatenate([dense_ref[at], dense_ref[at + 1]], axis=1)
                part = jnp.dot(back_ref[...], pair, preferred_element_type=F32).astype(BF16)
                ref[z] = part[:, :T]
                ref[z + 1] = part[:, T:]

    return pl.pallas_call(
        kernel,
        in_specs=[VMEM] * 2,
        out_specs=[VMEM] * 2,
        out_shape=[jax.ShapeDtypeStruct((Z, T, T), BF16)] * 2,
        compiler_params=params(16),
        name="backward",
    )(dense, back)


def bias_of(ref, start):
    return ref[start:start + 1, :].astype(F32) + ref[start + 1:start + 2, :].astype(F32)


def pair_sum(mine, theirs, keep, pay):
    def kernel(mine_ref, theirs_ref, keep_ref, pay_ref, out_ref):
        total = mine_ref[...].astype(F32) + theirs_ref[...].astype(F32)
        out_ref[:Z * T] = total.astype(BF16).reshape(Z * T, T)
        out_ref[Z * T:Z * T + HALF] = (keep_ref[:HALF] + pay_ref[:HALF].astype(F32)).astype(BF16)
        pack_bias(out_ref, Z * T + HALF, keep_ref[HALF:HALF + 1] + bias_of(pay_ref, HALF))

    return pl.pallas_call(
        kernel,
        in_specs=[VMEM] * 4,
        out_specs=VMEM,
        out_shape=jax.ShapeDtypeStruct((MSG, T), BF16),
        compiler_params=params(16),
        name="pair_sum",
    )(mine, theirs, keep, pay)


def line_sum(s0, s1, s2, s3):
    def kernel(r0, r1, r2, r3, out_ref):
        def add(a, b):
            get = lambda r: r[a:b].astype(F32)
            return (get(r0) + get(r2)) + (get(r1) + get(r3))

        terms = add(Z * T, Z * T + HALF).astype(BF16)
        at = Z * T + HALF
        bias = (bias_of(r0, at) + bias_of(r2, at)) + (bias_of(r1, at) + bias_of(r3, at))
        for z in range(Z):
            out_ref[z, :T] = add(z * T, z * T + T).astype(BF16)
            out_ref[z, T:T + HALF] = terms
            pack_bias(out_ref.at[z], T + HALF, bias)

    return pl.pallas_call(
        kernel,
        in_specs=[VMEM] * 4,
        out_specs=VMEM,
        out_shape=jax.ShapeDtypeStruct((Z, BLK, T), BF16),
        compiler_params=params(16),
        name="line_sum",
    )(s0, s1, s2, s3)


def finish(received):
    def kernel(in_ref, grad_ref, half_ref, bias_ref):
        total = in_ref[0, :T + HALF].astype(F32)
        bias = bias_of(in_ref.at[0], T + HALF)
        for z in range(1, Z):
            total += in_ref[z, :T + HALF].astype(F32)
            bias += bias_of(in_ref.at[z], T + HALF)
        grad_ref[...] = total[:T].T.astype(BF16)
        half_ref[...] = total[T:] * SCALE
        bias_ref[...] = bias * SCALE

    return pl.pallas_call(
        kernel,
        in_specs=[VMEM],
        out_specs=[VMEM] * 3,
        out_shape=[
            jax.ShapeDtypeStruct((T, T), BF16),
            jax.ShapeDtypeStruct((HALF, T), F32),
            jax.ShapeDtypeStruct((1, T), F32),
        ],
        compiler_params=params(16),
        name="finish",
    )(received)


def body(features, weight, bias_terms, cotangent, tile_values, tile_rows, tile_cols, tile_count):
    x, core, rep = lax.axis_index("x"), lax.axis_index("core"), lax.axis_index("rep")
    me = jnp.stack([x, core, rep]).astype(jnp.int32)
    cotangents = [cotangent] + [send(cotangent, "rep", Q, n) for n in range(1, Q)]

    spread = jnp.broadcast_to(features, (Z, T, T))
    line = lax.all_to_all(spread, "z", 0, 0, tiled=True)
    lines = [line] + [send(line, "x", X, n) for n in range(1, X)]
    gathered = []
    for block in lines:
        gathered += [block, send(block, "core", C, 1)]
    dense = densify(tile_rows[0, 0], tile_cols[0, 0], tile_count[0], me, tile_values[0, 0])
    partial = forward(dense, gathered)

    partials = [partial] + [send(partial, "rep", Q, n) for n in range(1, Q)]
    output, back, keep, pay = middle(me, partials, cotangents, weight, bias_terms.reshape(1, T))
    paid = send(pay, "core", C, 1)

    sums = {}
    for n in (2, 1, 3, 0):
        mine, theirs = backward(dense, back, n)
        theirs = send(theirs, "core", C, 1)
        total = pair_sum(mine, theirs, keep, paid)
        sums[n] = send(total, "x", X, -n) if n else total
    blocks = line_sum(sums[0], sums[1], sums[2], sums[3])
    received = lax.all_to_all(blocks, "z", 0, 0, tiled=True)
    grad_input, half, bias_grad = finish(received)
    other = send(half, "core", C, 1)
    weight_grad = jnp.where(core == 0, jnp.concatenate([half, other]), jnp.concatenate([other, half]))
    return output, grad_input, weight_grad, bias_grad.reshape(T)


def solution(mesh):
    fine = Mesh(mesh.devices.reshape(Z, X, C, Q), ALL)
    return jax.shard_map(
        body,
        mesh=fine,
        in_specs=(
            P(ALL, None),
            P(),
            P(),
            P(ALL, None),
            P(ROW, "rep", None, None, None),
            P(ROW, "rep", None),
            P(ROW, "rep", None),
            P(ROW, "rep"),
        ),
        out_specs=(P(ALL, None), P(ALL, None), P(), P()),
        check_vma=False,
    )
```

```python
import jax
import jax.numpy as jnp
from jax import lax
from jax.experimental import pallas as pl
from jax.experimental.pallas import tpu as pltpu
from jax.sharding import Mesh
from jax.sharding import PartitionSpec as P

Z, X, C, Q = 8, 4, 2, 4
T = 128
PANEL = Q * T
SLOTS = 128
PAY = T + 16
MSG = Z * T + PAY
BLK = T + PAY
F32 = jnp.float32
BF16 = jnp.bfloat16
ROW = ("z", "x", "core")
ALL = ("z", "x", "core", "rep")
SCALE = (Z * X * C * Q * T) ** -0.5

VMEM = pl.BlockSpec(memory_space=pltpu.VMEM)
SMEM = pl.BlockSpec(memory_space=pltpu.SMEM)


def params(mib):
    return pltpu.CompilerParams(vmem_limit_bytes=mib * 2**20)


def cost(flops, size):
    return pl.CostEstimate(flops=flops, bytes_accessed=size, transcendentals=0)


def shift(axis, size, by):
    return [(i, (i + by) % size) for i in range(size)]


def send(array, axis, size, by):
    return lax.ppermute(array, axis, shift(axis, size, by))


def densify_kernel(rows_ref, cols_ref, count_ref, me_ref, tiles_ref, dense_ref):
    def clear(p, carry):
        dense_ref[p] = jnp.zeros((PANEL, T), BF16)
        return carry

    lax.fori_loop(0, Z * X * C, clear, 0)
    x, core = me_ref[0], me_ref[1]

    def place(k, carry):
        col = cols_ref[k]
        z_col = col // (X * C)
        x_col = (col // C) % X
        core_col = col % C
        offset = (x - x_col + X) % X
        other = (core + core_col) % C
        position = (offset * C + other) * Z + z_col
        row = pl.multiple_of(rows_ref[k] * T, T)
        dense_ref[position, pl.ds(row, T), :] = tiles_ref[k]
        return carry

    lax.fori_loop(0, count_ref[0], place, 0)


def densify(rows, cols, count, me, tiles):
    return pl.pallas_call(
        densify_kernel,
        in_specs=[SMEM] * 4 + [VMEM],
        out_specs=VMEM,
        out_shape=jax.ShapeDtypeStruct((Z * X * C, PANEL, T), BF16),
        compiler_params=params(16),
        cost_estimate=cost(0, 12 * 2**20),
        name="densify",
    )(rows, cols, count, me, tiles)


def forward(dense, first, gathered, before=None, cotangent=None):
    last = before is not None
    count = len(gathered)

    def kernel(dense_ref, *refs):
        sources, out_ref, total = refs[:count], refs[-2], refs[-1]
        for n, source in enumerate(sources):
            panel = jnp.concatenate([dense_ref[(first + n) * Z + z] for z in range(Z)], axis=1)
            part = jnp.dot(panel, source[...].reshape(Z * T, T), preferred_element_type=F32)
            if n:
                part += total[...]
            elif last:
                part += refs[count][...]
            if n < count - 1:
                total[...] = part
            else:
                out_ref[:PANEL] = part.astype(out_ref.dtype)
        if last:
            out_ref[PANEL:] = refs[count + 1][...]

    extra = [before, cotangent] if last else []
    shape = jax.ShapeDtypeStruct((PANEL + T, T), BF16) if last else jax.ShapeDtypeStruct((PANEL, T), F32)
    return pl.pallas_call(
        kernel,
        in_specs=[VMEM] * (1 + count + len(extra)),
        out_specs=VMEM,
        out_shape=shape,
        scratch_shapes=[pltpu.VMEM((PANEL, T), F32)],
        compiler_params=params(16),
        cost_estimate=cost(2 * PANEL * T * T * Z * count, 2**20 * count),
        name="forward",
    )(dense, *gathered, *extra)


def tie(block, token):
    def kernel(block_ref, token_ref, out_ref):
        del block_ref, token_ref, out_ref

    return pl.pallas_call(
        kernel,
        in_specs=[VMEM] * 2,
        out_specs=VMEM,
        out_shape=jax.ShapeDtypeStruct(block.shape, block.dtype),
        input_output_aliases={0: 0},
        compiler_params=params(16),
        name="tie",
    )(block, token)


def split(value):
    high = value.astype(BF16)
    low = (value - high.astype(F32)).astype(BF16)
    return high, low


def pack_bias(ref, start, value):
    high, low = split(value)
    rows = lax.broadcasted_iota(jnp.int32, (16, T), 0)
    packed = jnp.where(rows == 0, high.astype(F32), jnp.where(rows == 1, low.astype(F32), 0.0))
    ref[start:start + 16, :] = packed.astype(BF16)


def middle_kernel(me_ref, p0, p1, p2, p3, weight_ref, bias_ref, out_ref, back_ref, pay_ref, pre, cot):
    rep = me_ref[2]
    for n, source in enumerate((p0, p1, p2, p3)):
        cot[(rep - n + Q) % Q] = source[PANEL:]
    get = lambda ref: ref[:PANEL].astype(F32)
    total = (get(p0) + get(p2)) + (get(p1) + get(p3))
    aggregated = total.astype(BF16)
    preact = jnp.dot(aggregated, weight_ref[...], preferred_element_type=F32) + bias_ref[...]
    pre[...] = preact.reshape(Q, T, T)
    sig = jax.nn.sigmoid(preact)
    cotangent = cot[...].reshape(PANEL, T).astype(F32)
    grad_pre = (cotangent * sig * (1.0 + preact * (1.0 - sig))).astype(BF16)
    own = pre[rep]
    out_ref[...] = (own * jax.nn.sigmoid(own)).astype(BF16)
    back = lax.dot_general(weight_ref[...], grad_pre, (((1,), (1,)), ((), ())), preferred_element_type=F32)
    back_ref[...] = back.astype(BF16)
    terms = lax.dot_general(aggregated, grad_pre, (((0,), (0,)), ((), ())), preferred_element_type=F32)
    bias_sum = jnp.sum(grad_pre.astype(F32), axis=0, keepdims=True)
    pay_ref[:T] = terms.astype(BF16)
    pack_bias(pay_ref, T, bias_sum)


def middle(me, partials, weight, bias):
    return pl.pallas_call(
        middle_kernel,
        in_specs=[SMEM] + [VMEM] * 6,
        out_specs=[VMEM] * 3,
        out_shape=[
            jax.ShapeDtypeStruct((T, T), BF16),
            jax.ShapeDtypeStruct((T, PANEL), BF16),
            jax.ShapeDtypeStruct((PAY, T), BF16),
        ],
        scratch_shapes=[pltpu.VMEM((Q, T, T), F32), pltpu.VMEM((Q, T, T), BF16)],
        compiler_params=params(16),
        cost_estimate=cost(6 * PANEL * T * T, 2**20),
        name="middle",
    )(me, *partials, weight, bias)


def backward(dense, back, chunk, pay=None):
    carries = pay is not None

    def kernel(dense_ref, back_ref, *refs):
        mine_ref, theirs_ref = refs[-2:]
        for n, ref in enumerate((mine_ref, theirs_ref)):
            for z in range(0, Z, 2):
                at = (chunk * C + n) * Z + z
                pair = jnp.concatenate([dense_ref[at], dense_ref[at + 1]], axis=1)
                part = jnp.dot(back_ref[...], pair, preferred_element_type=F32).astype(BF16)
                ref[z * T:z * T + T] = part[:, :T]
                ref[z * T + T:z * T + 2 * T] = part[:, T:]
        if carries:
            mine_ref[Z * T:] = refs[0][...]
            theirs_ref[Z * T:] = refs[0][...]

    rows = MSG if carries else Z * T
    extra = [pay] if carries else []
    return pl.pallas_call(
        kernel,
        in_specs=[VMEM] * (2 + len(extra)),
        out_specs=[VMEM] * 2,
        out_shape=[jax.ShapeDtypeStruct((rows, T), BF16)] * 2,
        compiler_params=params(16),
        cost_estimate=cost(2 * PANEL * T * T * Z * C, 2**21),
        name="backward",
    )(dense, back, *extra)


def bias_of(ref, start):
    pair = ref[start:start + 16, :].astype(F32)
    return pair[0:1] + pair[1:2]


def pair_sum(mine, theirs, pay=None):
    carried = pay is None

    def kernel(mine_ref, theirs_ref, *refs):
        out_ref = refs[-1]
        rows = Z * T + (T if carried else 0)
        total = mine_ref[:rows].astype(F32) + theirs_ref[:rows].astype(F32)
        out_ref[:rows] = total.astype(BF16)
        if carried:
            pack_bias(out_ref, rows, bias_of(mine_ref, rows) + bias_of(theirs_ref, rows))
        else:
            out_ref[rows:] = refs[0][rows:]

    extra = [] if carried else [pay]
    return pl.pallas_call(
        kernel,
        in_specs=[VMEM] * (2 + len(extra)),
        out_specs=VMEM,
        out_shape=jax.ShapeDtypeStruct((MSG, T), BF16),
        compiler_params=params(16),
        cost_estimate=cost(0, 2**20),
        name="pair_sum",
    )(mine, theirs, *extra)


def line_sum(s0, s1, s2, s3):
    def kernel(r0, r1, r2, r3, out_ref):
        def add(a, b):
            get = lambda r: r[a:b].astype(F32)
            return (get(r0) + get(r2)) + (get(r1) + get(r3))

        terms = add(Z * T, Z * T + T).astype(BF16)
        at = Z * T + T
        bias = (bias_of(r0, at) + bias_of(r2, at)) + (bias_of(r1, at) + bias_of(r3, at))
        for z in range(Z):
            out_ref[z, :T] = add(z * T, z * T + T).astype(BF16)
            out_ref[z, T:2 * T] = terms
            pack_bias(out_ref.at[z], 2 * T, bias)

    return pl.pallas_call(
        kernel,
        in_specs=[VMEM] * 4,
        out_specs=VMEM,
        out_shape=jax.ShapeDtypeStruct((Z, BLK, T), BF16),
        compiler_params=params(16),
        cost_estimate=cost(0, 2**20),
        name="line_sum",
    )(s0, s1, s2, s3)


def finish(received):
    def kernel(in_ref, grad_ref, weight_ref, bias_ref):
        total = in_ref[0, :2 * T].astype(F32)
        bias = bias_of(in_ref.at[0], 2 * T)
        for z in range(1, Z):
            total += in_ref[z, :2 * T].astype(F32)
            bias += bias_of(in_ref.at[z], 2 * T)
        grad_ref[...] = total[:T].T.astype(BF16)
        weight_ref[...] = total[T:] * SCALE
        bias_ref[...] = bias * SCALE

    return pl.pallas_call(
        kernel,
        in_specs=[VMEM],
        out_specs=[VMEM] * 3,
        out_shape=[
            jax.ShapeDtypeStruct((T, T), BF16),
            jax.ShapeDtypeStruct((T, T), F32),
            jax.ShapeDtypeStruct((1, T), F32),
        ],
        compiler_params=params(16),
        name="finish",
    )(received)


def body(features, weight, bias_terms, cotangent, tile_values, tile_rows, tile_cols, tile_count):
    x, core, rep = lax.axis_index("x"), lax.axis_index("core"), lax.axis_index("rep")
    me = jnp.stack([x, core, rep]).astype(jnp.int32)
    spread = jnp.broadcast_to(features, (Z, T, T))
    line = lax.all_to_all(spread, "z", 0, 0, tiled=True)
    dense = densify(tile_rows[0, 0], tile_cols[0, 0], tile_count[0], me, tile_values[0, 0])
    near = [line, send(line, "core", C, 1)]
    begun = forward(dense, 0, near)
    far = []
    for n in range(1, X):
        block = send(line, "x", X, n)
        if n > 1:
            block = tie(block, begun)
        far += [block, send(block, "core", C, 1)]
    partial = forward(dense, C, far, begun, cotangent)

    partials = [partial] + [send(partial, "rep", Q, n) for n in range(1, Q)]
    output, back, pay = middle(me, partials, weight, bias_terms.reshape(1, T))

    sums = {}
    for n in (1, 2, 3, 0):
        mine, theirs = backward(dense, back, n, pay if n == 1 else None)
        theirs = send(theirs, "core", C, 1)
        total = pair_sum(mine, theirs, None if n == 1 else first)
        if n == 1:
            first = total
        sums[n] = send(total, "x", X, -n) if n else total
    blocks = line_sum(sums[0], sums[1], sums[2], sums[3])
    received = lax.all_to_all(blocks, "z", 0, 0, tiled=True)
    grad_input, weight_grad, bias_grad = finish(received)
    return output, grad_input, weight_grad, bias_grad.reshape(T)


def solution(mesh):
    fine = Mesh(mesh.devices.reshape(Z, X, C, Q), ALL)
    return jax.shard_map(
        body,
        mesh=fine,
        in_specs=(
            P(ALL, None),
            P(),
            P(),
            P(ALL, None),
            P(ROW, "rep", None, None, None),
            P(ROW, "rep", None),
            P(ROW, "rep", None),
            P(ROW, "rep"),
        ),
        out_specs=(P(ALL, None), P(ALL, None), P(), P()),
        check_vma=False,
    )
```

```python
import jax
import jax.numpy as jnp
from jax import lax
from jax.experimental import pallas as pl
from jax.experimental.pallas import tpu as pltpu
from jax.sharding import Mesh
from jax.sharding import PartitionSpec as P

Z, X, C, Q = 8, 4, 2, 4
T = 128
PANEL = Q * T
SLOTS = 128
PAY = T + 16
MSG = Z * T + PAY
BLK = T + PAY
F32 = jnp.float32
BF16 = jnp.bfloat16
ROW = ("z", "x", "core")
ALL = ("z", "x", "core", "rep")
SCALE = (Z * X * C * Q * T) ** -0.5

VMEM = pl.BlockSpec(memory_space=pltpu.VMEM)
SMEM = pl.BlockSpec(memory_space=pltpu.SMEM)


def params(mib):
    return pltpu.CompilerParams(vmem_limit_bytes=mib * 2**20)


def cost(flops, size):
    return pl.CostEstimate(flops=flops, bytes_accessed=size, transcendentals=0)


def shift(axis, size, by):
    return [(i, (i + by) % size) for i in range(size)]


def send(array, axis, size, by):
    return lax.ppermute(array, axis, shift(axis, size, by))


def densify_kernel(rows_ref, cols_ref, count_ref, me_ref, tiles_ref, mine_ref, theirs_ref):
    def clear(p, carry):
        mine_ref[p] = jnp.zeros((PANEL, T), BF16)
        theirs_ref[p] = jnp.zeros((PANEL, T), BF16)
        return carry

    lax.fori_loop(0, Z * X, clear, 0)
    x, core = me_ref[0], me_ref[1]

    def place(k, carry):
        col = cols_ref[k]
        offset = (x - (col >> 1) + X) & (X - 1)
        at = offset * Z + (col >> 3)
        span = pl.ds(pl.multiple_of(rows_ref[k] * T, T), T)
        own = (col & 1) == core

        @pl.when(own)
        def _():
            mine_ref[at, span, :] = tiles_ref[k]

        @pl.when(jnp.logical_not(own))
        def _():
            theirs_ref[at, span, :] = tiles_ref[k]

        return carry

    lax.fori_loop(0, count_ref[0], place, 0)


def densify(rows, cols, count, me, tiles):
    return pl.pallas_call(
        densify_kernel,
        in_specs=[SMEM] * 4 + [VMEM],
        out_specs=[VMEM] * 2,
        out_shape=[jax.ShapeDtypeStruct((Z * X, PANEL, T), BF16)] * 2,
        compiler_params=params(16),
        cost_estimate=cost(0, 12 * 2**20),
        name="densify",
    )(rows, cols, count, me, tiles)


def forward(halves, sources, before, dtype, rider=None):
    count = len(sources)
    places = [(half, n) for half, n, _ in sources]
    extra = [array for array in (before, rider) if array is not None]

    def kernel(*refs):
        out_ref, total = refs[-2:]
        for i, (half, n) in enumerate(places):
            panel = jnp.concatenate([refs[half][n * Z + z] for z in range(Z)], axis=1)
            part = jnp.dot(panel, refs[2 + i][...].reshape(Z * T, T), preferred_element_type=F32)
            if i:
                part += total[...]
            elif before is not None:
                part += refs[2 + count][...]
            if i < count - 1:
                total[...] = part
            else:
                out_ref[:PANEL] = part.astype(dtype)
        if rider is not None:
            out_ref[PANEL:] = refs[3 + count][...]

    return pl.pallas_call(
        kernel,
        in_specs=[VMEM] * (2 + count + len(extra)),
        out_specs=VMEM,
        out_shape=jax.ShapeDtypeStruct((PANEL if rider is None else PANEL + T, T), dtype),
        scratch_shapes=[pltpu.VMEM((PANEL, T), F32)],
        compiler_params=params(16),
        cost_estimate=cost(2 * PANEL * T * T * Z * count, 2**20 * count),
        name="forward",
    )(*halves, *(block for _, _, block in sources), *extra)


def tie(block, token):
    def kernel(block_ref, token_ref, out_ref):
        del block_ref, token_ref, out_ref

    return pl.pallas_call(
        kernel,
        in_specs=[VMEM] * 2,
        out_specs=VMEM,
        out_shape=jax.ShapeDtypeStruct(block.shape, block.dtype),
        input_output_aliases={0: 0},
        compiler_params=params(16),
        name="tie",
    )(block, token)


def split(value):
    high = value.astype(BF16)
    low = (value - high.astype(F32)).astype(BF16)
    return high, low


def pack_bias(ref, start, value):
    high, low = split(value)
    rows = lax.broadcasted_iota(jnp.int32, (16, T), 0)
    packed = jnp.where(rows == 0, high.astype(F32), jnp.where(rows == 1, low.astype(F32), 0.0))
    ref[start:start + 16, :] = packed.astype(BF16)


def middle_kernel(me_ref, p0, p1, p2, p3, weight_ref, bias_ref, out_ref, give_ref, pre, cot):
    rep = me_ref[2]
    for n, source in enumerate((p0, p1, p2, p3)):
        cot[(rep - n + Q) % Q] = source[PANEL:]
    get = lambda ref: ref[:PANEL].astype(F32)
    total = (get(p0) + get(p2)) + (get(p1) + get(p3))
    aggregated = total.astype(BF16)
    preact = jnp.dot(aggregated, weight_ref[...], preferred_element_type=F32) + bias_ref[...]
    pre[...] = preact.reshape(Q, T, T)
    sig = jax.nn.sigmoid(preact)
    cotangent = cot[...].reshape(PANEL, T).astype(F32)
    grad_pre = (cotangent * sig * (1.0 + preact * (1.0 - sig))).astype(BF16)
    own = pre[rep]
    out_ref[...] = (own * jax.nn.sigmoid(own)).astype(BF16)
    back = lax.dot_general(weight_ref[...], grad_pre, (((1,), (1,)), ((), ())), preferred_element_type=F32)
    for r in range(Q):
        give_ref[r * T:(r + 1) * T] = back[:, r * T:(r + 1) * T].astype(BF16)
    terms = lax.dot_general(aggregated, grad_pre, (((0,), (0,)), ((), ())), preferred_element_type=F32)
    bias_sum = jnp.sum(grad_pre.astype(F32), axis=0, keepdims=True)
    give_ref[PANEL:PANEL + T] = terms.astype(BF16)
    pack_bias(give_ref, PANEL + T, bias_sum)


def middle(me, partials, weight, bias):
    return pl.pallas_call(
        middle_kernel,
        in_specs=[SMEM] + [VMEM] * 6,
        out_specs=[VMEM] * 2,
        out_shape=[
            jax.ShapeDtypeStruct((T, T), BF16),
            jax.ShapeDtypeStruct((PANEL + PAY, T), BF16),
        ],
        scratch_shapes=[pltpu.VMEM((Q, T, T), F32), pltpu.VMEM((Q, T, T), BF16)],
        compiler_params=params(16),
        cost_estimate=cost(6 * PANEL * T * T, 2**20),
        name="middle",
    )(me, *partials, weight, bias)


def bias_of(ref, start):
    pair = ref[start:start + 16, :].astype(F32)
    return pair[0:1] + pair[1:2]


def backward(mine, other, give, got, chunk):
    def kernel(mine_ref, other_ref, give_ref, got_ref, out_ref):
        wide = lambda ref: jnp.concatenate([ref[r * T:(r + 1) * T] for r in range(Q)], axis=1)
        sides = [(wide(give_ref), mine_ref), (wide(got_ref), other_ref)]
        for z in range(0, Z, 2):
            at = chunk * Z + z
            part = None
            for back, ref in sides:
                pair = jnp.concatenate([ref[at], ref[at + 1]], axis=1)
                term = jnp.dot(back, pair, preferred_element_type=F32)
                part = term if part is None else part + term
            part = part.astype(BF16)
            out_ref[z * T:z * T + T] = part[:, :T]
            out_ref[z * T + T:z * T + 2 * T] = part[:, T:]
        terms = give_ref[PANEL:PANEL + T].astype(F32) + got_ref[PANEL:PANEL + T].astype(F32)
        out_ref[Z * T:Z * T + T] = terms.astype(BF16)
        pack_bias(out_ref, Z * T + T, bias_of(give_ref, PANEL + T) + bias_of(got_ref, PANEL + T))

    return pl.pallas_call(
        kernel,
        in_specs=[VMEM] * 4,
        out_specs=VMEM,
        out_shape=jax.ShapeDtypeStruct((MSG, T), BF16),
        compiler_params=params(16),
        cost_estimate=cost(4 * PANEL * T * T * Z, 2**21),
        name="backward",
    )(mine, other, give, got)


def line_sum(s0, s1, s2, s3):
    def kernel(r0, r1, r2, r3, out_ref):
        def add(a, b):
            get = lambda r: r[a:b].astype(F32)
            return (get(r0) + get(r2)) + (get(r1) + get(r3))

        terms = add(Z * T, Z * T + T).astype(BF16)
        at = Z * T + T
        bias = (bias_of(r0, at) + bias_of(r2, at)) + (bias_of(r1, at) + bias_of(r3, at))
        for z in range(Z):
            out_ref[z, :T] = add(z * T, z * T + T).astype(BF16)
            out_ref[z, T:2 * T] = terms
            pack_bias(out_ref.at[z], 2 * T, bias)

    return pl.pallas_call(
        kernel,
        in_specs=[VMEM] * 4,
        out_specs=VMEM,
        out_shape=jax.ShapeDtypeStruct((Z, BLK, T), BF16),
        compiler_params=params(16),
        cost_estimate=cost(0, 2**20),
        name="line_sum",
    )(s0, s1, s2, s3)


def finish(received):
    def kernel(in_ref, grad_ref, weight_ref, bias_ref):
        total = in_ref[0, :2 * T].astype(F32)
        bias = bias_of(in_ref.at[0], 2 * T)
        for z in range(1, Z):
            total += in_ref[z, :2 * T].astype(F32)
            bias += bias_of(in_ref.at[z], 2 * T)
        grad_ref[...] = total[:T].T.astype(BF16)
        weight_ref[...] = total[T:] * SCALE
        bias_ref[...] = bias * SCALE

    return pl.pallas_call(
        kernel,
        in_specs=[VMEM],
        out_specs=[VMEM] * 3,
        out_shape=[
            jax.ShapeDtypeStruct((T, T), BF16),
            jax.ShapeDtypeStruct((T, T), F32),
            jax.ShapeDtypeStruct((1, T), F32),
        ],
        compiler_params=params(16),
        name="finish",
    )(received)


def body(features, weight, bias_terms, cotangent, tile_values, tile_rows, tile_cols, tile_count):
    x, core, rep = lax.axis_index("x"), lax.axis_index("core"), lax.axis_index("rep")
    me = jnp.stack([x, core, rep]).astype(jnp.int32)
    spread = jnp.broadcast_to(features, (Z, T, T))
    line = lax.all_to_all(spread, "z", 0, 0, tiled=True)
    halves = densify(tile_rows[0, 0], tile_cols[0, 0], tile_count[0], me, tile_values[0, 0])
    near = [(0, 0, line), (1, 0, send(line, "core", C, 1))]
    begun = forward(halves, near, None, F32)
    far = []
    for n in range(1, X):
        block = send(line, "x", X, n)
        if n > 1:
            block = tie(block, begun)
        far += [(0, n, block), (1, n, send(block, "core", C, 1))]
    begun = forward(halves, far[:-1], begun, F32)
    partial = forward(halves, far[-1:], begun, BF16, cotangent)

    partials = [partial] + [send(partial, "rep", Q, n) for n in range(1, Q)]
    mine, theirs = halves
    other = send(tie(theirs, partial), "core", C, 1)
    output, give = middle(me, partials, weight, bias_terms.reshape(1, T))
    got = send(give, "core", C, 1)

    sums = {}
    for n in (1, 2, 3, 0):
        total = backward(mine, other, give, got, n)
        sums[n] = send(total, "x", X, -n) if n else total
    blocks = line_sum(sums[0], sums[1], sums[2], sums[3])
    received = lax.all_to_all(blocks, "z", 0, 0, tiled=True)
    grad_input, weight_grad, bias_grad = finish(received)
    return output, grad_input, weight_grad, bias_grad.reshape(T)


def solution(mesh):
    fine = Mesh(mesh.devices.reshape(Z, X, C, Q), ALL)
    return jax.shard_map(
        body,
        mesh=fine,
        in_specs=(
            P(ALL, None),
            P(),
            P(),
            P(ALL, None),
            P(ROW, "rep", None, None, None),
            P(ROW, "rep", None),
            P(ROW, "rep", None),
            P(ROW, "rep"),
        ),
        out_specs=(P(ALL, None), P(ALL, None), P(), P()),
        check_vma=False,
    )
```

```python
import jax
import jax.numpy as jnp
from jax import lax
from jax.experimental import pallas as pl
from jax.experimental.pallas import tpu as pltpu
from jax.sharding import Mesh
from jax.sharding import PartitionSpec as P

Z, X, C, Q = 8, 4, 2, 4
T = 128
PANEL = Q * T
SLOTS = 128
HALF = T // 2
PAY = HALF + 16
MSG = Z * T + PAY
BLK = T + PAY
F32 = jnp.float32
BF16 = jnp.bfloat16
ROW = ("z", "x", "core")
ALL = ("z", "x", "core", "rep")
SCALE = (Z * X * C * Q * T) ** -0.5

VMEM = pl.BlockSpec(memory_space=pltpu.VMEM)
SMEM = pl.BlockSpec(memory_space=pltpu.SMEM)


def params(mib):
    return pltpu.CompilerParams(vmem_limit_bytes=mib * 2**20)


def cost(flops, size):
    return pl.CostEstimate(flops=flops, bytes_accessed=size, transcendentals=0)


def shift(axis, size, by):
    return [(i, (i + by) % size) for i in range(size)]


def send(array, axis, size, by):
    return lax.ppermute(array, axis, shift(axis, size, by))


def densify_kernel(me_ref, tiles_ref, mine_ref, theirs_ref):
    def clear(p, carry):
        mine_ref[p] = jnp.zeros((PANEL, T), BF16)
        theirs_ref[p] = jnp.zeros((PANEL, T), BF16)
        return carry

    lax.fori_loop(0, Z * X, clear, 0)
    x, core = me_ref[0], me_ref[1]

    def place(k, carry):
        col = me_ref[4 + SLOTS + k]
        offset = (x - (col >> 1) + X) & (X - 1)
        at = offset * Z + (col >> 3)
        span = pl.ds(pl.multiple_of(me_ref[4 + k] * T, T), T)
        own = (col & 1) == core

        @pl.when(own)
        def _():
            mine_ref[at, span, :] = tiles_ref[k]

        @pl.when(jnp.logical_not(own))
        def _():
            theirs_ref[at, span, :] = tiles_ref[k]

        return carry

    lax.fori_loop(0, me_ref[3], place, 0)


def densify(me, tiles):
    return pl.pallas_call(
        densify_kernel,
        in_specs=[SMEM, VMEM],
        out_specs=[VMEM] * 2,
        out_shape=[jax.ShapeDtypeStruct((Z * X, PANEL, T), BF16)] * 2,
        compiler_params=params(16),
        cost_estimate=cost(0, 12 * 2**20),
        name="densify",
    )(me, tiles)


def forward(halves, sources, before, dtype, rider=None):
    count = len(sources)
    places = [(half, n) for half, n, _ in sources]
    extra = [array for array in (before, rider) if array is not None]

    def kernel(*refs):
        out_ref, total = refs[-2:]
        for i, (half, n) in enumerate(places):
            panel = jnp.concatenate([refs[half][n * Z + z] for z in range(Z)], axis=1)
            part = jnp.dot(panel, refs[2 + i][...].reshape(Z * T, T), preferred_element_type=F32)
            if i:
                part += total[...]
            elif before is not None:
                part += refs[2 + count][...]
            if i < count - 1:
                total[...] = part
            else:
                out_ref[:PANEL] = part.astype(dtype)
        if rider is not None:
            out_ref[PANEL:] = refs[3 + count][...]

    return pl.pallas_call(
        kernel,
        in_specs=[VMEM] * (2 + count + len(extra)),
        out_specs=VMEM,
        out_shape=jax.ShapeDtypeStruct((PANEL if rider is None else PANEL + T, T), dtype),
        scratch_shapes=[pltpu.VMEM((PANEL, T), F32)],
        compiler_params=params(16),
        cost_estimate=cost(2 * PANEL * T * T * Z * count, 2**20 * count),
        name="forward",
    )(*halves, *(block for _, _, block in sources), *extra)


def tie(block, token):
    def kernel(block_ref, token_ref, out_ref):
        del block_ref, token_ref, out_ref

    return pl.pallas_call(
        kernel,
        in_specs=[VMEM] * 2,
        out_specs=VMEM,
        out_shape=jax.ShapeDtypeStruct(block.shape, block.dtype),
        input_output_aliases={0: 0},
        compiler_params=params(16),
        name="tie",
    )(block, token)


def split(value):
    high = value.astype(BF16)
    low = (value - high.astype(F32)).astype(BF16)
    return high, low


def pack_bias(ref, start, value):
    high, low = split(value)
    rows = lax.broadcasted_iota(jnp.int32, (16, T), 0)
    packed = jnp.where(rows == 0, high.astype(F32), jnp.where(rows == 1, low.astype(F32), 0.0))
    ref[start:start + 16, :] = packed.astype(BF16)


def middle_kernel(me_ref, p0, p1, p2, p3, weight_ref, bias_ref, out_ref, give_ref, keep_ref, pre, cot, halves):
    core, rep = me_ref[1], me_ref[2]
    for n, source in enumerate((p0, p1, p2, p3)):
        cot[(rep - n + Q) % Q] = source[PANEL:]
    get = lambda ref: ref[:PANEL].astype(F32)
    total = (get(p0) + get(p2)) + (get(p1) + get(p3))
    aggregated = total.astype(BF16)
    preact = jnp.dot(aggregated, weight_ref[...], preferred_element_type=F32) + bias_ref[...]
    pre[...] = preact.reshape(Q, T, T)
    sig = jax.nn.sigmoid(preact)
    cotangent = cot[...].reshape(PANEL, T).astype(F32)
    grad_pre = (cotangent * sig * (1.0 + preact * (1.0 - sig))).astype(BF16)
    own = pre[rep]
    out_ref[...] = (own * jax.nn.sigmoid(own)).astype(BF16)
    back = lax.dot_general(weight_ref[...], grad_pre, (((1,), (1,)), ((), ())), preferred_element_type=F32)
    for r in range(Q):
        give_ref[r * T:(r + 1) * T] = back[:, r * T:(r + 1) * T].astype(BF16)
    terms = lax.dot_general(aggregated, grad_pre, (((0,), (0,)), ((), ())), preferred_element_type=F32)
    bias_sum = jnp.sum(grad_pre.astype(F32), axis=0, keepdims=True)
    halves[...] = terms.reshape(C, HALF, T)
    keep_ref[...] = halves[core]
    give_ref[PANEL:PANEL + HALF] = halves[1 - core].astype(BF16)
    pack_bias(give_ref, PANEL + HALF, bias_sum)


def middle(me, partials, weight, bias):
    return pl.pallas_call(
        middle_kernel,
        in_specs=[SMEM] + [VMEM] * 6,
        out_specs=[VMEM] * 3,
        out_shape=[
            jax.ShapeDtypeStruct((T, T), BF16),
            jax.ShapeDtypeStruct((PANEL + PAY, T), BF16),
            jax.ShapeDtypeStruct((HALF, T), F32),
        ],
        scratch_shapes=[
            pltpu.VMEM((Q, T, T), F32),
            pltpu.VMEM((Q, T, T), BF16),
            pltpu.VMEM((C, HALF, T), F32),
        ],
        compiler_params=params(16),
        cost_estimate=cost(6 * PANEL * T * T, 2**20),
        name="middle",
    )(me, *partials, weight, bias)


def bias_of(ref, start):
    pair = ref[start:start + 16, :].astype(F32)
    return pair[0:1] + pair[1:2]


def backward(mine, other, give, got, keep, chunk):
    def kernel(mine_ref, other_ref, give_ref, got_ref, keep_ref, out_ref):
        wide = lambda ref: jnp.concatenate([ref[r * T:(r + 1) * T] for r in range(Q)], axis=1)
        sides = [(wide(give_ref), mine_ref), (wide(got_ref), other_ref)]
        for z in range(0, Z, 2):
            at = chunk * Z + z
            part = None
            for back, ref in sides:
                pair = jnp.concatenate([ref[at], ref[at + 1]], axis=1)
                term = jnp.dot(back, pair, preferred_element_type=F32)
                part = term if part is None else part + term
            part = part.astype(BF16)
            out_ref[z * T:z * T + T] = part[:, :T]
            out_ref[z * T + T:z * T + 2 * T] = part[:, T:]
        terms = keep_ref[...] + got_ref[PANEL:PANEL + HALF].astype(F32)
        out_ref[Z * T:Z * T + HALF] = terms.astype(BF16)
        bias = bias_of(give_ref, PANEL + HALF) + bias_of(got_ref, PANEL + HALF)
        pack_bias(out_ref, Z * T + HALF, bias)

    return pl.pallas_call(
        kernel,
        in_specs=[VMEM] * 5,
        out_specs=VMEM,
        out_shape=jax.ShapeDtypeStruct((MSG, T), BF16),
        compiler_params=params(16),
        cost_estimate=cost(4 * PANEL * T * T * Z, 2**21),
        name="backward",
    )(mine, other, give, got, keep)


def line_sum(s0, s1, s2, s3):
    def kernel(r0, r1, r2, r3, out_ref):
        def add(a, b):
            get = lambda r: r[a:b].astype(F32)
            return (get(r0) + get(r2)) + (get(r1) + get(r3))

        terms = add(Z * T, Z * T + HALF).astype(BF16)
        at = Z * T + HALF
        bias = (bias_of(r0, at) + bias_of(r2, at)) + (bias_of(r1, at) + bias_of(r3, at))
        for z in range(Z):
            out_ref[z, :T] = add(z * T, z * T + T).astype(BF16)
            out_ref[z, T:T + HALF] = terms
            pack_bias(out_ref.at[z], T + HALF, bias)

    return pl.pallas_call(
        kernel,
        in_specs=[VMEM] * 4,
        out_specs=VMEM,
        out_shape=jax.ShapeDtypeStruct((Z, BLK, T), BF16),
        compiler_params=params(16),
        cost_estimate=cost(0, 2**20),
        name="line_sum",
    )(s0, s1, s2, s3)


def finish_terms(received):
    def kernel(in_ref, half_ref, bias_ref):
        total = in_ref[0, T:T + HALF].astype(F32)
        bias = bias_of(in_ref.at[0], T + HALF)
        for z in range(1, Z):
            total += in_ref[z, T:T + HALF].astype(F32)
            bias += bias_of(in_ref.at[z], T + HALF)
        half_ref[...] = total * SCALE
        bias_ref[...] = bias * SCALE

    return pl.pallas_call(
        kernel,
        in_specs=[VMEM],
        out_specs=[VMEM] * 2,
        out_shape=[
            jax.ShapeDtypeStruct((HALF, T), F32),
            jax.ShapeDtypeStruct((1, T), F32),
        ],
        compiler_params=params(16),
        cost_estimate=cost(0, 2**18),
        name="finish_terms",
    )(received)


def finish_grad(received):
    def kernel(in_ref, grad_ref):
        total = in_ref[0, :T].astype(F32)
        for z in range(1, Z):
            total += in_ref[z, :T].astype(F32)
        grad_ref[...] = total.T.astype(BF16)

    return pl.pallas_call(
        kernel,
        in_specs=[VMEM],
        out_specs=VMEM,
        out_shape=jax.ShapeDtypeStruct((T, T), BF16),
        compiler_params=params(16),
        cost_estimate=cost(0, 2**22),
        name="finish_grad",
    )(received)


def body(features, weight, bias_terms, cotangent, tile_values, tile_rows, tile_cols, tile_count):
    x, core, rep = lax.axis_index("x"), lax.axis_index("core"), lax.axis_index("rep")
    place = jnp.stack([x, core, rep, tile_count[0, 0]]).astype(jnp.int32)
    me = jnp.concatenate([place, tile_rows[0, 0], tile_cols[0, 0]])
    spread = jnp.broadcast_to(features, (Z, T, T))
    line = lax.all_to_all(spread, "z", 0, 0, tiled=True)
    halves = densify(me, tile_values[0, 0])
    near = [(0, 0, line), (1, 0, send(line, "core", C, 1))]
    begun = forward(halves, near, None, F32)
    far = []
    for n in range(1, X):
        block = send(line, "x", X, n)
        if n > 1:
            block = tie(block, begun)
        far += [(0, n, block), (1, n, send(block, "core", C, 1))]
    begun = forward(halves, far[:-1], begun, F32)
    partial = forward(halves, far[-1:], begun, BF16, cotangent)

    partials = [partial] + [send(partial, "rep", Q, n) for n in range(1, Q)]
    mine, theirs = halves
    fellow = send(tie(theirs, partial), "core", C, 1)
    output, give, keep = middle(place, partials, weight, bias_terms.reshape(1, T))
    got = send(give, "core", C, 1)

    sums = {}
    for n in (1, 2, 3, 0):
        total = backward(mine, fellow, give, got, keep, n)
        sums[n] = send(total, "x", X, -n) if n else total
    blocks = line_sum(sums[0], sums[1], sums[2], sums[3])
    received = lax.all_to_all(blocks, "z", 0, 0, tiled=True)
    half, bias_grad = finish_terms(received)
    other = send(half, "core", C, 1)
    weight_grad = jnp.where(core == 0, jnp.concatenate([half, other]), jnp.concatenate([other, half]))
    grad_input = finish_grad(received)
    return output, grad_input, weight_grad, bias_grad.reshape(T)


def solution(mesh):
    fine = Mesh(mesh.devices.reshape(Z, X, C, Q), ALL)
    return jax.shard_map(
        body,
        mesh=fine,
        in_specs=(
            P(ALL, None),
            P(),
            P(),
            P(ALL, None),
            P(ROW, "rep", None, None, None),
            P(ROW, "rep", None),
            P(ROW, "rep", None),
            P(ROW, "rep"),
        ),
        out_specs=(P(ALL, None), P(ALL, None), P(), P()),
        check_vma=False,
    )
```

```python
import jax
import jax.numpy as jnp
from jax import lax
from jax.experimental import pallas as pl
from jax.experimental.pallas import tpu as pltpu
from jax.sharding import Mesh
from jax.sharding import PartitionSpec as P

Z, X, C, Q = 8, 4, 2, 4
T = 128
PANEL = Q * T
SLOTS = 128
HALF = T // 2
PAY = HALF + 16
MSG = Z * T + PAY
BLK = T + PAY
F32 = jnp.float32
BF16 = jnp.bfloat16
ROW = ("z", "x", "core")
ALL = ("z", "x", "core", "rep")
SCALE = (Z * X * C * Q * T) ** -0.5

VMEM = pl.BlockSpec(memory_space=pltpu.VMEM)
SMEM = pl.BlockSpec(memory_space=pltpu.SMEM)


def params(mib):
    return pltpu.CompilerParams(vmem_limit_bytes=mib * 2**20)


def cost(flops, size):
    return pl.CostEstimate(flops=flops, bytes_accessed=size, transcendentals=0)


def shift(axis, size, by):
    return [(i, (i + by) % size) for i in range(size)]


def send(array, axis, size, by):
    return lax.ppermute(array, axis, shift(axis, size, by))


def densify_kernel(me_ref, tiles_ref, mine_ref, theirs_ref):
    def clear(p, carry):
        mine_ref[p] = jnp.zeros((PANEL, T), BF16)
        theirs_ref[p] = jnp.zeros((PANEL, T), BF16)
        return carry

    lax.fori_loop(0, Z * X, clear, 0)
    x, core = me_ref[0], me_ref[1]

    def place(k, carry):
        col = me_ref[4 + SLOTS + k]
        offset = (x - (col >> 1) + X) & (X - 1)
        at = offset * Z + (col >> 3)
        span = pl.ds(pl.multiple_of(me_ref[4 + k] * T, T), T)
        own = (col & 1) == core

        @pl.when(own)
        def _():
            mine_ref[at, span, :] = tiles_ref[k]

        @pl.when(jnp.logical_not(own))
        def _():
            theirs_ref[at, span, :] = tiles_ref[k]

        return carry

    lax.fori_loop(0, me_ref[3], place, 0)


def densify(me, tiles):
    return pl.pallas_call(
        densify_kernel,
        in_specs=[SMEM, VMEM],
        out_specs=[VMEM] * 2,
        out_shape=[jax.ShapeDtypeStruct((Z * X, PANEL, T), BF16)] * 2,
        compiler_params=params(16),
        cost_estimate=cost(0, 12 * 2**20),
        name="densify",
    )(me, tiles)


def forward(halves, sources, before, dtype, rider=None):
    count = len(sources)
    places = [(half, n) for half, n, _ in sources]
    extra = [array for array in (before, rider) if array is not None]

    def kernel(*refs):
        out_ref, total = refs[-2:]
        for i, (half, n) in enumerate(places):
            panel = jnp.concatenate([refs[half][n * Z + z] for z in range(Z)], axis=1)
            part = jnp.dot(panel, refs[2 + i][...].reshape(Z * T, T), preferred_element_type=F32)
            if i:
                part += total[...]
            elif before is not None:
                part += refs[2 + count][...]
            if i < count - 1:
                total[...] = part
            else:
                out_ref[:PANEL] = part.astype(dtype)
        if rider is not None:
            out_ref[PANEL:] = refs[3 + count][...]

    return pl.pallas_call(
        kernel,
        in_specs=[VMEM] * (2 + count + len(extra)),
        out_specs=VMEM,
        out_shape=jax.ShapeDtypeStruct((PANEL if rider is None else PANEL + T, T), dtype),
        scratch_shapes=[pltpu.VMEM((PANEL, T), F32)],
        compiler_params=params(16),
        cost_estimate=cost(2 * PANEL * T * T * Z * count, 2**20 * count),
        name="forward",
    )(*halves, *(block for _, _, block in sources), *extra)


def tie(block, token):
    def kernel(block_ref, token_ref, out_ref):
        del block_ref, token_ref, out_ref

    return pl.pallas_call(
        kernel,
        in_specs=[VMEM] * 2,
        out_specs=VMEM,
        out_shape=jax.ShapeDtypeStruct(block.shape, block.dtype),
        input_output_aliases={0: 0},
        compiler_params=params(16),
        name="tie",
    )(block, token)


def split(value):
    high = value.astype(BF16)
    low = (value - high.astype(F32)).astype(BF16)
    return high, low


def pack_bias(ref, start, value):
    high, low = split(value)
    rows = lax.broadcasted_iota(jnp.int32, (16, T), 0)
    packed = jnp.where(rows == 0, high.astype(F32), jnp.where(rows == 1, low.astype(F32), 0.0))
    ref[start:start + 16, :] = packed.astype(BF16)


def middle_kernel(me_ref, p0, p1, p2, p3, weight_ref, bias_ref, own_ref, give_ref, keep_ref, pre, cot, halves):
    core, rep = me_ref[1], me_ref[2]
    for n, source in enumerate((p0, p1, p2, p3)):
        cot[(rep - n + Q) % Q] = source[PANEL:]
    get = lambda ref: ref[:PANEL].astype(F32)
    total = (get(p0) + get(p2)) + (get(p1) + get(p3))
    aggregated = total.astype(BF16)
    preact = jnp.dot(aggregated, weight_ref[...], preferred_element_type=F32) + bias_ref[...]
    pre[...] = preact.reshape(Q, T, T)
    sig = jax.nn.sigmoid(preact)
    cotangent = cot[...].reshape(PANEL, T).astype(F32)
    grad_pre = (cotangent * sig * (1.0 + preact * (1.0 - sig))).astype(BF16)
    own_ref[...] = pre[rep]
    back = lax.dot_general(weight_ref[...], grad_pre, (((1,), (1,)), ((), ())), preferred_element_type=F32)
    for r in range(Q):
        give_ref[r * T:(r + 1) * T] = back[:, r * T:(r + 1) * T].astype(BF16)
    terms = lax.dot_general(aggregated, grad_pre, (((0,), (0,)), ((), ())), preferred_element_type=F32)
    bias_sum = jnp.sum(grad_pre.astype(F32), axis=0, keepdims=True)
    halves[...] = terms.reshape(C, HALF, T)
    keep_ref[...] = halves[core]
    give_ref[PANEL:PANEL + HALF] = halves[1 - core].astype(BF16)
    pack_bias(give_ref, PANEL + HALF, bias_sum)


def middle(me, partials, weight, bias):
    return pl.pallas_call(
        middle_kernel,
        in_specs=[SMEM] + [VMEM] * 6,
        out_specs=[VMEM] * 3,
        out_shape=[
            jax.ShapeDtypeStruct((T, T), F32),
            jax.ShapeDtypeStruct((PANEL + PAY, T), BF16),
            jax.ShapeDtypeStruct((HALF, T), F32),
        ],
        scratch_shapes=[
            pltpu.VMEM((Q, T, T), F32),
            pltpu.VMEM((Q, T, T), BF16),
            pltpu.VMEM((C, HALF, T), F32),
        ],
        compiler_params=params(16),
        cost_estimate=cost(6 * PANEL * T * T, 2**20),
        name="middle",
    )(me, *partials, weight, bias)


def bias_of(ref, start):
    pair = ref[start:start + 16, :].astype(F32)
    return pair[0:1] + pair[1:2]


def backward(mine, other, give, got, keep, chunk, own=None):
    def kernel(mine_ref, other_ref, give_ref, got_ref, keep_ref, *refs):
        if own is None:
            out_ref, = refs
        else:
            own_ref, out_ref, layer_ref = refs
            preact = own_ref[...]
            layer_ref[...] = (preact * jax.nn.sigmoid(preact)).astype(BF16)
        wide = lambda ref: jnp.concatenate([ref[r * T:(r + 1) * T] for r in range(Q)], axis=1)
        sides = [(wide(give_ref), mine_ref), (wide(got_ref), other_ref)]
        for z in range(0, Z, 2):
            at = chunk * Z + z
            part = None
            for back, ref in sides:
                pair = jnp.concatenate([ref[at], ref[at + 1]], axis=1)
                term = jnp.dot(back, pair, preferred_element_type=F32)
                part = term if part is None else part + term
            part = part.astype(BF16)
            out_ref[z * T:z * T + T] = part[:, :T]
            out_ref[z * T + T:z * T + 2 * T] = part[:, T:]
        terms = keep_ref[...] + got_ref[PANEL:PANEL + HALF].astype(F32)
        out_ref[Z * T:Z * T + HALF] = terms.astype(BF16)
        bias = bias_of(give_ref, PANEL + HALF) + bias_of(got_ref, PANEL + HALF)
        pack_bias(out_ref, Z * T + HALF, bias)

    extra = [] if own is None else [own]
    return pl.pallas_call(
        kernel,
        in_specs=[VMEM] * (5 + len(extra)),
        out_specs=[VMEM] * (1 + len(extra)),
        out_shape=[jax.ShapeDtypeStruct((MSG, T), BF16)] + [jax.ShapeDtypeStruct((T, T), BF16)] * len(extra),
        compiler_params=params(16),
        cost_estimate=cost(4 * PANEL * T * T * Z, 2**21),
        name="backward",
    )(mine, other, give, got, keep, *extra)


def line_sum(s0, s1, s2, s3):
    def kernel(r0, r1, r2, r3, out_ref):
        def add(a, b):
            get = lambda r: r[a:b].astype(F32)
            return (get(r0) + get(r2)) + (get(r1) + get(r3))

        terms = add(Z * T, Z * T + HALF).astype(BF16)
        at = Z * T + HALF
        bias = (bias_of(r0, at) + bias_of(r2, at)) + (bias_of(r1, at) + bias_of(r3, at))
        for z in range(Z):
            out_ref[z, :T] = add(z * T, z * T + T).astype(BF16)
            out_ref[z, T:T + HALF] = terms
            pack_bias(out_ref.at[z], T + HALF, bias)

    return pl.pallas_call(
        kernel,
        in_specs=[VMEM] * 4,
        out_specs=VMEM,
        out_shape=jax.ShapeDtypeStruct((Z, BLK, T), BF16),
        compiler_params=params(16),
        cost_estimate=cost(0, 2**20),
        name="line_sum",
    )(s0, s1, s2, s3)


def finish_terms(received):
    def kernel(in_ref, half_ref):
        total = in_ref[0, T:T + HALF].astype(F32)
        for z in range(1, Z):
            total += in_ref[z, T:T + HALF].astype(F32)
        half_ref[...] = total * SCALE

    return pl.pallas_call(
        kernel,
        in_specs=[VMEM],
        out_specs=VMEM,
        out_shape=jax.ShapeDtypeStruct((HALF, T), F32),
        compiler_params=params(16),
        cost_estimate=cost(0, 2**18),
        name="finish_terms",
    )(received)


def finish_grad(received):
    def kernel(in_ref, grad_ref, bias_ref):
        total = in_ref[0, :T].astype(F32)
        bias = bias_of(in_ref.at[0], T + HALF)
        for z in range(1, Z):
            total += in_ref[z, :T].astype(F32)
            bias += bias_of(in_ref.at[z], T + HALF)
        grad_ref[...] = total.T.astype(BF16)
        bias_ref[...] = bias * SCALE

    return pl.pallas_call(
        kernel,
        in_specs=[VMEM],
        out_specs=[VMEM] * 2,
        out_shape=[
            jax.ShapeDtypeStruct((T, T), BF16),
            jax.ShapeDtypeStruct((1, T), F32),
        ],
        compiler_params=params(16),
        cost_estimate=cost(0, 2**22),
        name="finish_grad",
    )(received)


def body(features, weight, bias_terms, cotangent, tile_values, tile_rows, tile_cols, tile_count):
    x, core, rep = lax.axis_index("x"), lax.axis_index("core"), lax.axis_index("rep")
    place = jnp.stack([x, core, rep, tile_count[0, 0]]).astype(jnp.int32)
    me = jnp.concatenate([place, tile_rows[0, 0], tile_cols[0, 0]])
    spread = jnp.broadcast_to(features, (Z, T, T))
    line = lax.all_to_all(spread, "z", 0, 0, tiled=True)
    halves = densify(me, tile_values[0, 0])
    near = [(0, 0, line), (1, 0, send(line, "core", C, 1))]
    begun = forward(halves, near, None, F32)
    far = []
    for n in range(1, X):
        block = tie(send(line, "x", X, n), begun)
        far += [(0, n, block), (1, n, send(block, "core", C, 1))]
    late = [far[3], far[5]]
    begun = forward(halves, far[:3] + far[4:5], begun, F32)
    partial = forward(halves, late, begun, BF16, cotangent)

    partials = [partial] + [send(partial, "rep", Q, n) for n in range(1, Q)]
    mine, theirs = halves
    fellow = send(tie(theirs, partial), "core", C, 1)
    own, give, keep = middle(place, partials, weight, bias_terms.reshape(1, T))
    got = send(give, "core", C, 1)

    sums = {}
    for n in (1, 2, 3):
        total, = backward(mine, fellow, give, got, keep, n)
        sums[n] = send(total, "x", X, -n)
    sums[0], output = backward(mine, fellow, give, got, keep, 0, own)
    blocks = line_sum(sums[0], sums[3], sums[2], sums[1])
    received = lax.all_to_all(blocks, "z", 0, 0, tiled=True)
    half = finish_terms(received)
    other = send(half, "core", C, 1)
    weight_grad = jnp.where(core == 0, jnp.concatenate([half, other]), jnp.concatenate([other, half]))
    grad_input, bias_grad = finish_grad(received)
    return output, grad_input, weight_grad, bias_grad.reshape(T)


def solution(mesh):
    fine = Mesh(mesh.devices.reshape(Z, X, C, Q), ALL)
    return jax.shard_map(
        body,
        mesh=fine,
        in_specs=(
            P(ALL, None),
            P(),
            P(),
            P(ALL, None),
            P(ROW, "rep", None, None, None),
            P(ROW, "rep", None),
            P(ROW, "rep", None),
            P(ROW, "rep"),
        ),
        out_specs=(P(ALL, None), P(ALL, None), P(), P()),
        check_vma=False,
    )
```

```python
import jax
import jax.numpy as jnp
from jax import lax
from jax.experimental import pallas as pl
from jax.experimental.pallas import tpu as pltpu
from jax.sharding import Mesh
from jax.sharding import PartitionSpec as P

Z, X, C, Q = 8, 4, 2, 4
T = 128
PANEL = Q * T
SLOTS = 128
HALF = T // 2
PAY = HALF + 16
MSG = Z * T + PAY
BLK = T + PAY
F32 = jnp.float32
BF16 = jnp.bfloat16
ROW = ("z", "x", "core")
ALL = ("z", "x", "core", "rep")
SCALE = (Z * X * C * Q * T) ** -0.5

VMEM = pl.BlockSpec(memory_space=pltpu.VMEM)
SMEM = pl.BlockSpec(memory_space=pltpu.SMEM)


def params(mib):
    return pltpu.CompilerParams(vmem_limit_bytes=mib * 2**20)


def cost(flops, size):
    return pl.CostEstimate(flops=flops, bytes_accessed=size, transcendentals=0)


def shift(axis, size, by):
    return [(i, (i + by) % size) for i in range(size)]


def send(array, axis, size, by):
    return lax.ppermute(array, axis, shift(axis, size, by))


def densify_kernel(me_ref, tiles_ref, mine_ref, theirs_ref):
    def clear(p, carry):
        mine_ref[p] = jnp.zeros((PANEL, T), BF16)
        theirs_ref[p] = jnp.zeros((PANEL, T), BF16)
        return carry

    lax.fori_loop(0, Z * X, clear, 0)
    x, core = me_ref[0], me_ref[1]

    def place(k, carry):
        col = me_ref[4 + SLOTS + k]
        offset = (x - (col >> 1) + X) & (X - 1)
        at = offset * Z + (col >> 3)
        span = pl.ds(pl.multiple_of(me_ref[4 + k] * T, T), T)
        own = (col & 1) == core

        @pl.when(own)
        def _():
            mine_ref[at, span, :] = tiles_ref[k]

        @pl.when(jnp.logical_not(own))
        def _():
            theirs_ref[at, span, :] = tiles_ref[k]

        return carry

    lax.fori_loop(0, me_ref[3], place, 0)


def densify(me, tiles):
    return pl.pallas_call(
        densify_kernel,
        in_specs=[SMEM, VMEM],
        out_specs=[VMEM] * 2,
        out_shape=[jax.ShapeDtypeStruct((Z * X, PANEL, T), BF16)] * 2,
        compiler_params=params(16),
        cost_estimate=cost(0, 12 * 2**20),
        name="densify",
    )(me, tiles)


def forward(halves, sources, before, dtype, rider=None):
    count = len(sources)
    places = [(half, n) for half, n, _ in sources]
    extra = [array for array in (before, rider) if array is not None]

    def kernel(*refs):
        out_ref, total = refs[-2:]
        for i, (half, n) in enumerate(places):
            panel = jnp.concatenate([refs[half][n * Z + z] for z in range(Z)], axis=1)
            part = jnp.dot(panel, refs[2 + i][...].reshape(Z * T, T), preferred_element_type=F32)
            if i:
                part += total[...]
            elif before is not None:
                part += refs[2 + count][...]
            if i < count - 1:
                total[...] = part
            else:
                out_ref[:PANEL] = part.astype(dtype)
        if rider is not None:
            out_ref[PANEL:] = refs[3 + count][...]

    return pl.pallas_call(
        kernel,
        in_specs=[VMEM] * (2 + count + len(extra)),
        out_specs=VMEM,
        out_shape=jax.ShapeDtypeStruct((PANEL if rider is None else PANEL + T, T), dtype),
        scratch_shapes=[pltpu.VMEM((PANEL, T), F32)],
        compiler_params=params(16),
        cost_estimate=cost(2 * PANEL * T * T * Z * count, 2**20 * count),
        name="forward",
    )(*halves, *(block for _, _, block in sources), *extra)


def tie(block, token):
    def kernel(block_ref, token_ref, out_ref):
        del block_ref, token_ref, out_ref

    return pl.pallas_call(
        kernel,
        in_specs=[VMEM] * 2,
        out_specs=VMEM,
        out_shape=jax.ShapeDtypeStruct(block.shape, block.dtype),
        input_output_aliases={0: 0},
        compiler_params=params(16),
        name="tie",
    )(block, token)


def split(value):
    high = value.astype(BF16)
    low = (value - high.astype(F32)).astype(BF16)
    return high, low


def pack_bias(ref, start, value):
    high, low = split(value)
    rows = lax.broadcasted_iota(jnp.int32, (16, T), 0)
    packed = jnp.where(rows == 0, high.astype(F32), jnp.where(rows == 1, low.astype(F32), 0.0))
    ref[start:start + 16, :] = packed.astype(BF16)


def middle_kernel(me_ref, p0, p1, p2, p3, weight_ref, bias_ref, own_ref, give_ref, keep_ref, pre, cot, halves):
    core, rep = me_ref[1], me_ref[2]
    for n, source in enumerate((p0, p1, p2, p3)):
        cot[(rep - n + Q) % Q] = source[PANEL:]
    get = lambda ref: ref[:PANEL].astype(F32)
    total = (get(p0) + get(p2)) + (get(p1) + get(p3))
    aggregated = total.astype(BF16)
    preact = jnp.dot(aggregated, weight_ref[...], preferred_element_type=F32) + bias_ref[...]
    pre[...] = preact.reshape(Q, T, T)
    sig = jax.nn.sigmoid(preact)
    cotangent = cot[...].reshape(PANEL, T).astype(F32)
    grad_pre = (cotangent * sig * (1.0 + preact * (1.0 - sig))).astype(BF16)
    own_ref[...] = pre[rep]
    back = lax.dot_general(weight_ref[...], grad_pre, (((1,), (1,)), ((), ())), preferred_element_type=F32)
    for r in range(Q):
        give_ref[r * T:(r + 1) * T] = back[:, r * T:(r + 1) * T].astype(BF16)
    terms = lax.dot_general(aggregated, grad_pre, (((0,), (0,)), ((), ())), preferred_element_type=F32)
    bias_sum = jnp.sum(grad_pre.astype(F32), axis=0, keepdims=True)
    halves[...] = terms.reshape(C, HALF, T)
    keep_ref[...] = halves[core]
    give_ref[PANEL:PANEL + HALF] = halves[1 - core].astype(BF16)
    pack_bias(give_ref, PANEL + HALF, bias_sum)


def middle(me, partials, weight, bias):
    return pl.pallas_call(
        middle_kernel,
        in_specs=[SMEM] + [VMEM] * 6,
        out_specs=[VMEM] * 3,
        out_shape=[
            jax.ShapeDtypeStruct((T, T), F32),
            jax.ShapeDtypeStruct((PANEL + PAY, T), BF16),
            jax.ShapeDtypeStruct((HALF, T), F32),
        ],
        scratch_shapes=[
            pltpu.VMEM((Q, T, T), F32),
            pltpu.VMEM((Q, T, T), BF16),
            pltpu.VMEM((C, HALF, T), F32),
        ],
        compiler_params=params(16),
        cost_estimate=cost(6 * PANEL * T * T, 2**20),
        name="middle",
    )(me, *partials, weight, bias)


def bias_of(ref, start):
    pair = ref[start:start + 16, :].astype(F32)
    return pair[0:1] + pair[1:2]


def wide(ref):
    return jnp.concatenate([ref[r * T:(r + 1) * T] for r in range(Q)], axis=1)


def products(back, panels_ref, chunk, z):
    at = chunk * Z + z
    pair = jnp.concatenate([panels_ref[at], panels_ref[at + 1]], axis=1)
    return jnp.dot(back, pair, preferred_element_type=F32)


def backward_own(mine, give):
    def kernel(mine_ref, give_ref, out_ref):
        back = wide(give_ref)

        def step(chunk, carry):
            for z in range(0, Z, 2):
                part = products(back, mine_ref, chunk, z)
                out_ref[chunk, z] = part[:, :T]
                out_ref[chunk, z + 1] = part[:, T:]
            return carry

        lax.fori_loop(0, X, step, 0)

    return pl.pallas_call(
        kernel,
        in_specs=[VMEM] * 2,
        out_specs=VMEM,
        out_shape=jax.ShapeDtypeStruct((X, Z, T, T), F32),
        compiler_params=params(16),
        cost_estimate=cost(2 * PANEL * T * T * Z * X, 2**22),
        name="backward_own",
    )(mine, give)


def backward(begun, other, give, got, keep, chunk, own=None):
    def kernel(begun_ref, other_ref, give_ref, got_ref, keep_ref, *refs):
        if own is None:
            out_ref, = refs
        else:
            own_ref, out_ref, layer_ref = refs
            preact = own_ref[...]
            layer_ref[...] = (preact * jax.nn.sigmoid(preact)).astype(BF16)
        back = wide(got_ref)
        for z in range(0, Z, 2):
            part = products(back, other_ref, chunk, z)
            out_ref[z * T:z * T + T] = (begun_ref[chunk, z] + part[:, :T]).astype(BF16)
            out_ref[z * T + T:z * T + 2 * T] = (begun_ref[chunk, z + 1] + part[:, T:]).astype(BF16)
        terms = keep_ref[...] + got_ref[PANEL:PANEL + HALF].astype(F32)
        out_ref[Z * T:Z * T + HALF] = terms.astype(BF16)
        bias = bias_of(give_ref, PANEL + HALF) + bias_of(got_ref, PANEL + HALF)
        pack_bias(out_ref, Z * T + HALF, bias)

    extra = [] if own is None else [own]
    return pl.pallas_call(
        kernel,
        in_specs=[VMEM] * (5 + len(extra)),
        out_specs=[VMEM] * (1 + len(extra)),
        out_shape=[jax.ShapeDtypeStruct((MSG, T), BF16)] + [jax.ShapeDtypeStruct((T, T), BF16)] * len(extra),
        compiler_params=params(16),
        cost_estimate=cost(2 * PANEL * T * T * Z, 2**21),
        name="backward",
    )(begun, other, give, got, keep, *extra)


def line_sum(s0, s1, s2, s3):
    def kernel(r0, r1, r2, r3, out_ref):
        def add(a, b):
            get = lambda r: r[a:b].astype(F32)
            return (get(r0) + get(r2)) + (get(r1) + get(r3))

        terms = add(Z * T, Z * T + HALF).astype(BF16)
        at = Z * T + HALF
        bias = (bias_of(r0, at) + bias_of(r2, at)) + (bias_of(r1, at) + bias_of(r3, at))
        for z in range(Z):
            out_ref[z, :T] = add(z * T, z * T + T).astype(BF16)
            out_ref[z, T:T + HALF] = terms
            pack_bias(out_ref.at[z], T + HALF, bias)

    return pl.pallas_call(
        kernel,
        in_specs=[VMEM] * 4,
        out_specs=VMEM,
        out_shape=jax.ShapeDtypeStruct((Z, BLK, T), BF16),
        compiler_params=params(16),
        cost_estimate=cost(0, 2**20),
        name="line_sum",
    )(s0, s1, s2, s3)


def finish_terms(received):
    def kernel(in_ref, half_ref):
        total = in_ref[0, T:T + HALF].astype(F32)
        for z in range(1, Z):
            total += in_ref[z, T:T + HALF].astype(F32)
        half_ref[...] = total * SCALE

    return pl.pallas_call(
        kernel,
        in_specs=[VMEM],
        out_specs=VMEM,
        out_shape=jax.ShapeDtypeStruct((HALF, T), F32),
        compiler_params=params(16),
        cost_estimate=cost(0, 2**18),
        name="finish_terms",
    )(received)


def finish_grad(received):
    def kernel(in_ref, grad_ref, bias_ref):
        total = in_ref[0, :T].astype(F32)
        bias = bias_of(in_ref.at[0], T + HALF)
        for z in range(1, Z):
            total += in_ref[z, :T].astype(F32)
            bias += bias_of(in_ref.at[z], T + HALF)
        grad_ref[...] = total.T.astype(BF16)
        bias_ref[...] = bias * SCALE

    return pl.pallas_call(
        kernel,
        in_specs=[VMEM],
        out_specs=[VMEM] * 2,
        out_shape=[
            jax.ShapeDtypeStruct((T, T), BF16),
            jax.ShapeDtypeStruct((1, T), F32),
        ],
        compiler_params=params(16),
        cost_estimate=cost(0, 2**22),
        name="finish_grad",
    )(received)


def body(features, weight, bias_terms, cotangent, tile_values, tile_rows, tile_cols, tile_count):
    x, core, rep = lax.axis_index("x"), lax.axis_index("core"), lax.axis_index("rep")
    place = jnp.stack([x, core, rep, tile_count[0, 0]]).astype(jnp.int32)
    me = jnp.concatenate([place, tile_rows[0, 0], tile_cols[0, 0]])
    spread = jnp.broadcast_to(features, (Z, T, T))
    line = lax.all_to_all(spread, "z", 0, 0, tiled=True)
    halves = densify(me, tile_values[0, 0])
    begun = forward(halves, [(0, 0, line)], None, F32)
    near = [(1, 0, send(line, "core", C, 1))]
    far = []
    for n in range(1, X):
        block = tie(send(line, "x", X, n), begun)
        far += [(0, n, block), (1, n, send(block, "core", C, 1))]
    late = [far[3], far[5]]
    begun = forward(halves, near + far[:3] + far[4:5], begun, F32)
    partial = forward(halves, late, begun, BF16, cotangent)

    partials = [partial] + [send(partial, "rep", Q, n) for n in range(1, Q)]
    mine, theirs = halves
    fellow = send(tie(theirs, partial), "core", C, 1)
    own, give, keep = middle(place, partials, weight, bias_terms.reshape(1, T))
    got = send(give, "core", C, 1)

    ahead = backward_own(mine, give)
    sums = {}
    for n in (1, 2, 3):
        total, = backward(ahead, fellow, give, got, keep, n)
        sums[n] = send(total, "x", X, -n)
    sums[0], output = backward(ahead, fellow, give, got, keep, 0, own)
    blocks = line_sum(sums[0], sums[3], sums[2], sums[1])
    received = lax.all_to_all(blocks, "z", 0, 0, tiled=True)
    half = finish_terms(received)
    other = send(half, "core", C, 1)
    weight_grad = jnp.where(core == 0, jnp.concatenate([half, other]), jnp.concatenate([other, half]))
    grad_input, bias_grad = finish_grad(received)
    return output, grad_input, weight_grad, bias_grad.reshape(T)


def solution(mesh):
    fine = Mesh(mesh.devices.reshape(Z, X, C, Q), ALL)
    return jax.shard_map(
        body,
        mesh=fine,
        in_specs=(
            P(ALL, None),
            P(),
            P(),
            P(ALL, None),
            P(ROW, "rep", None, None, None),
            P(ROW, "rep", None),
            P(ROW, "rep", None),
            P(ROW, "rep"),
        ),
        out_specs=(P(ALL, None), P(ALL, None), P(), P()),
        check_vma=False,
    )
```

```python
import jax
import jax.numpy as jnp
from jax import lax
from jax.experimental import pallas as pl
from jax.experimental.pallas import tpu as pltpu
from jax.sharding import Mesh
from jax.sharding import PartitionSpec as P

Z, X, C, Q = 8, 4, 2, 4
T = 128
PANEL = Q * T
SLOTS = 128
HALF = T // 2
PAY = HALF + 16
MSG = Z * T + PAY
BLK = T + PAY
F32 = jnp.float32
BF16 = jnp.bfloat16
ROW = ("z", "x", "core")
ALL = ("z", "x", "core", "rep")
SCALE = (Z * X * C * Q * T) ** -0.5

VMEM = pl.BlockSpec(memory_space=pltpu.VMEM)
SMEM = pl.BlockSpec(memory_space=pltpu.SMEM)


def params(mib):
    return pltpu.CompilerParams(vmem_limit_bytes=mib * 2**20)


def cost(flops, size):
    return pl.CostEstimate(flops=flops, bytes_accessed=size, transcendentals=0)


def shift(axis, size, by):
    return [(i, (i + by) % size) for i in range(size)]


def send(array, axis, size, by):
    return lax.ppermute(array, axis, shift(axis, size, by))


def densify_kernel(me_ref, tiles_ref, mine_ref, theirs_ref):
    def clear(p, carry):
        mine_ref[p] = jnp.zeros((PANEL, T), BF16)
        theirs_ref[p] = jnp.zeros((PANEL, T), BF16)
        return carry

    lax.fori_loop(0, Z * X, clear, 0)
    def place(k, carry):
        at = me_ref[4 + SLOTS + k]
        span = pl.ds(pl.multiple_of(me_ref[4 + k], T), T)

        @pl.when(at < Z * X)
        def _():
            mine_ref[at, span, :] = tiles_ref[k]

        @pl.when(at >= Z * X)
        def _():
            theirs_ref[at - Z * X, span, :] = tiles_ref[k]

        return carry

    lax.fori_loop(0, me_ref[3], place, 0)


def densify(me, tiles):
    return pl.pallas_call(
        densify_kernel,
        in_specs=[SMEM, VMEM],
        out_specs=[VMEM] * 2,
        out_shape=[jax.ShapeDtypeStruct((Z * X, PANEL, T), BF16)] * 2,
        compiler_params=params(16),
        cost_estimate=cost(0, 12 * 2**20),
        name="densify",
    )(me, tiles)


def forward(halves, sources, before, dtype, rider=None):
    count = len(sources)
    places = [(half, n) for half, n, _ in sources]
    extra = [array for array in (before, rider) if array is not None]

    def kernel(*refs):
        out_ref, total = refs[-2:]
        for i, (half, n) in enumerate(places):
            panel = jnp.concatenate([refs[half][n * Z + z] for z in range(Z)], axis=1)
            part = jnp.dot(panel, refs[2 + i][...].reshape(Z * T, T), preferred_element_type=F32)
            if i:
                part += total[...]
            elif before is not None:
                part += refs[2 + count][...]
            if i < count - 1:
                total[...] = part
            else:
                out_ref[:PANEL] = part.astype(dtype)
        if rider is not None:
            out_ref[PANEL:] = refs[3 + count][...]

    return pl.pallas_call(
        kernel,
        in_specs=[VMEM] * (2 + count + len(extra)),
        out_specs=VMEM,
        out_shape=jax.ShapeDtypeStruct((PANEL if rider is None else PANEL + T, T), dtype),
        scratch_shapes=[pltpu.VMEM((PANEL, T), F32)],
        compiler_params=params(16),
        cost_estimate=cost(2 * PANEL * T * T * Z * count, 2**20 * count),
        name="forward",
    )(*halves, *(block for _, _, block in sources), *extra)


def tie(block, token):
    def kernel(block_ref, token_ref, out_ref):
        del block_ref, token_ref, out_ref

    return pl.pallas_call(
        kernel,
        in_specs=[VMEM] * 2,
        out_specs=VMEM,
        out_shape=jax.ShapeDtypeStruct(block.shape, block.dtype),
        input_output_aliases={0: 0},
        compiler_params=params(16),
        name="tie",
    )(block, token)


def split(value):
    high = value.astype(BF16)
    low = (value - high.astype(F32)).astype(BF16)
    return high, low


def pack_bias(ref, start, value):
    high, low = split(value)
    rows = lax.broadcasted_iota(jnp.int32, (16, T), 0)
    packed = jnp.where(rows == 0, high.astype(F32), jnp.where(rows == 1, low.astype(F32), 0.0))
    ref[start:start + 16, :] = packed.astype(BF16)


def middle_kernel(me_ref, p0, p1, p2, p3, weight_ref, bias_ref, own_ref, give_ref, keep_ref, pre, cot, halves):
    core, rep = me_ref[1], me_ref[2]
    for n, source in enumerate((p0, p1, p2, p3)):
        cot[(rep - n + Q) % Q] = source[PANEL:]
    get = lambda ref: ref[:PANEL].astype(F32)
    total = (get(p0) + get(p2)) + (get(p1) + get(p3))
    aggregated = total.astype(BF16)
    preact = jnp.dot(aggregated, weight_ref[...], preferred_element_type=F32) + bias_ref[...]
    pre[...] = preact.reshape(Q, T, T)
    sig = jax.nn.sigmoid(preact)
    cotangent = cot[...].reshape(PANEL, T).astype(F32)
    grad_pre = (cotangent * sig * (1.0 + preact * (1.0 - sig))).astype(BF16)
    own_ref[...] = pre[rep]
    back = lax.dot_general(weight_ref[...], grad_pre, (((1,), (1,)), ((), ())), preferred_element_type=F32)
    for r in range(Q):
        give_ref[r * T:(r + 1) * T] = back[:, r * T:(r + 1) * T].astype(BF16)
    terms = lax.dot_general(aggregated, grad_pre, (((0,), (0,)), ((), ())), preferred_element_type=F32)
    bias_sum = jnp.sum(grad_pre.astype(F32), axis=0, keepdims=True)
    halves[...] = terms.reshape(C, HALF, T)
    keep_ref[...] = halves[core]
    give_ref[PANEL:PANEL + HALF] = halves[1 - core].astype(BF16)
    pack_bias(give_ref, PANEL + HALF, bias_sum)


def middle(me, partials, weight, bias):
    return pl.pallas_call(
        middle_kernel,
        in_specs=[SMEM] + [VMEM] * 6,
        out_specs=[VMEM] * 3,
        out_shape=[
            jax.ShapeDtypeStruct((T, T), F32),
            jax.ShapeDtypeStruct((PANEL + PAY, T), BF16),
            jax.ShapeDtypeStruct((HALF, T), F32),
        ],
        scratch_shapes=[
            pltpu.VMEM((Q, T, T), F32),
            pltpu.VMEM((Q, T, T), BF16),
            pltpu.VMEM((C, HALF, T), F32),
        ],
        compiler_params=params(16),
        cost_estimate=cost(6 * PANEL * T * T, 2**20),
        name="middle",
    )(me, *partials, weight, bias)


def bias_of(ref, start):
    pair = ref[start:start + 16, :].astype(F32)
    return pair[0:1] + pair[1:2]


def wide(ref):
    return jnp.concatenate([ref[r * T:(r + 1) * T] for r in range(Q)], axis=1)


def products(back, panels_ref, chunk, z):
    at = chunk * Z + z
    pair = jnp.concatenate([panels_ref[at], panels_ref[at + 1]], axis=1)
    return jnp.dot(back, pair, preferred_element_type=F32)


def backward_own(mine, give):
    def kernel(mine_ref, give_ref, out_ref):
        back = wide(give_ref)

        def step(chunk, carry):
            for z in range(0, Z, 2):
                part = products(back, mine_ref, chunk, z)
                out_ref[chunk, z] = part[:, :T]
                out_ref[chunk, z + 1] = part[:, T:]
            return carry

        lax.fori_loop(0, X, step, 0)

    return pl.pallas_call(
        kernel,
        in_specs=[VMEM] * 2,
        out_specs=VMEM,
        out_shape=jax.ShapeDtypeStruct((X, Z, T, T), F32),
        compiler_params=params(16),
        cost_estimate=cost(2 * PANEL * T * T * Z * X, 2**22),
        name="backward_own",
    )(mine, give)


def backward(begun, other, give, got, keep, chunk, own=None):
    def kernel(begun_ref, other_ref, give_ref, got_ref, keep_ref, *refs):
        if own is None:
            out_ref, = refs
        else:
            own_ref, out_ref, layer_ref = refs
            preact = own_ref[...]
            layer_ref[...] = (preact * jax.nn.sigmoid(preact)).astype(BF16)
        back = wide(got_ref)
        for z in range(0, Z, 2):
            part = products(back, other_ref, chunk, z)
            out_ref[z * T:z * T + T] = (begun_ref[chunk, z] + part[:, :T]).astype(BF16)
            out_ref[z * T + T:z * T + 2 * T] = (begun_ref[chunk, z + 1] + part[:, T:]).astype(BF16)
        terms = keep_ref[...] + got_ref[PANEL:PANEL + HALF].astype(F32)
        out_ref[Z * T:Z * T + HALF] = terms.astype(BF16)
        bias = bias_of(give_ref, PANEL + HALF) + bias_of(got_ref, PANEL + HALF)
        pack_bias(out_ref, Z * T + HALF, bias)

    extra = [] if own is None else [own]
    return pl.pallas_call(
        kernel,
        in_specs=[VMEM] * (5 + len(extra)),
        out_specs=[VMEM] * (1 + len(extra)),
        out_shape=[jax.ShapeDtypeStruct((MSG, T), BF16)] + [jax.ShapeDtypeStruct((T, T), BF16)] * len(extra),
        compiler_params=params(16),
        cost_estimate=cost(2 * PANEL * T * T * Z, 2**21),
        name="backward",
    )(begun, other, give, got, keep, *extra)


def line_sum(s0, s1, s2, s3):
    def kernel(r0, r1, r2, r3, out_ref):
        def add(a, b):
            get = lambda r: r[a:b].astype(F32)
            return (get(r0) + get(r2)) + (get(r1) + get(r3))

        terms = add(Z * T, Z * T + HALF).astype(BF16)
        at = Z * T + HALF
        bias = (bias_of(r0, at) + bias_of(r2, at)) + (bias_of(r1, at) + bias_of(r3, at))
        for z in range(Z):
            out_ref[z, :T] = add(z * T, z * T + T).astype(BF16)
            out_ref[z, T:T + HALF] = terms
            pack_bias(out_ref.at[z], T + HALF, bias)

    return pl.pallas_call(
        kernel,
        in_specs=[VMEM] * 4,
        out_specs=VMEM,
        out_shape=jax.ShapeDtypeStruct((Z, BLK, T), BF16),
        compiler_params=params(16),
        cost_estimate=cost(0, 2**20),
        name="line_sum",
    )(s0, s1, s2, s3)


def finish_terms(received):
    def kernel(in_ref, half_ref):
        total = in_ref[0, T:T + HALF].astype(F32)
        for z in range(1, Z):
            total += in_ref[z, T:T + HALF].astype(F32)
        half_ref[...] = total * SCALE

    return pl.pallas_call(
        kernel,
        in_specs=[VMEM],
        out_specs=VMEM,
        out_shape=jax.ShapeDtypeStruct((HALF, T), F32),
        compiler_params=params(16),
        cost_estimate=cost(0, 2**18),
        name="finish_terms",
    )(received)


def finish_grad(received):
    def kernel(in_ref, grad_ref, bias_ref):
        total = in_ref[0, :T].astype(F32)
        bias = bias_of(in_ref.at[0], T + HALF)
        for z in range(1, Z):
            total += in_ref[z, :T].astype(F32)
            bias += bias_of(in_ref.at[z], T + HALF)
        grad_ref[...] = total.T.astype(BF16)
        bias_ref[...] = bias * SCALE

    return pl.pallas_call(
        kernel,
        in_specs=[VMEM],
        out_specs=[VMEM] * 2,
        out_shape=[
            jax.ShapeDtypeStruct((T, T), BF16),
            jax.ShapeDtypeStruct((1, T), F32),
        ],
        compiler_params=params(16),
        cost_estimate=cost(0, 2**22),
        name="finish_grad",
    )(received)


def body(features, weight, bias_terms, cotangent, tile_values, tile_rows, tile_cols, tile_count):
    x, core, rep = lax.axis_index("x"), lax.axis_index("core"), lax.axis_index("rep")
    place = jnp.stack([x, core, rep, tile_count[0, 0]]).astype(jnp.int32)
    cols = tile_cols[0, 0]
    half = (cols & 1) ^ core.astype(jnp.int32)
    offset = (x.astype(jnp.int32) - (cols >> 1)) & (X - 1)
    at = (half * X + offset) * Z + (cols >> 3)
    me = jnp.concatenate([place, tile_rows[0, 0] * T, at])
    spread = jnp.broadcast_to(features, (Z, T, T))
    line = lax.all_to_all(spread, "z", 0, 0, tiled=True)
    halves = densify(me, tile_values[0, 0])
    near = [(0, 0, line), (1, 0, send(line, "core", C, 1))]
    far = []
    for n in range(1, X):
        block = tie(send(line, "x", X, n), halves[0])
        far += [(0, n, block), (1, n, send(block, "core", C, 1))]
    late = [far[3], far[5]]
    begun = forward(halves, near + far[:3] + far[4:5], None, F32)
    partial = forward(halves, late, begun, BF16, cotangent)

    partials = [partial] + [send(partial, "rep", Q, n) for n in range(1, Q)]
    mine, theirs = halves
    fellow = send(tie(theirs, partial), "core", C, 1)
    own, give, keep = middle(place, partials, weight, bias_terms.reshape(1, T))
    got = send(give, "core", C, 1)

    ahead = backward_own(mine, give)
    sums = {}
    for n in (1, 2, 3):
        total, = backward(ahead, fellow, give, got, keep, n)
        sums[n] = send(total, "x", X, -n)
    sums[0], output = backward(ahead, fellow, give, got, keep, 0, own)
    blocks = line_sum(sums[0], sums[3], sums[2], sums[1])
    received = lax.all_to_all(blocks, "z", 0, 0, tiled=True)
    half = finish_terms(received)
    other = send(half, "core", C, 1)
    weight_grad = jnp.where(core == 0, jnp.concatenate([half, other]), jnp.concatenate([other, half]))
    grad_input, bias_grad = finish_grad(received)
    return output, grad_input, weight_grad, bias_grad.reshape(T)


def solution(mesh):
    fine = Mesh(mesh.devices.reshape(Z, X, C, Q), ALL)
    return jax.shard_map(
        body,
        mesh=fine,
        in_specs=(
            P(ALL, None),
            P(),
            P(),
            P(ALL, None),
            P(ROW, "rep", None, None, None),
            P(ROW, "rep", None),
            P(ROW, "rep", None),
            P(ROW, "rep"),
        ),
        out_specs=(P(ALL, None), P(ALL, None), P(), P()),
        check_vma=False,
    )
```

```python
import jax
import jax.numpy as jnp
from jax import lax
from jax.experimental import pallas as pl
from jax.experimental.pallas import tpu as pltpu
from jax.sharding import Mesh
from jax.sharding import PartitionSpec as P

Z, X, C, Q = 8, 4, 2, 4
T = 128
PANEL = Q * T
SLOTS = 128
HALF = T // 2
PAY = HALF + 16
MSG = Z * T + PAY
BLK = T + PAY
F32 = jnp.float32
BF16 = jnp.bfloat16
ROW = ("z", "x", "core")
ALL = ("z", "x", "core", "rep")
SCALE = (Z * X * C * Q * T) ** -0.5

VMEM = pl.BlockSpec(memory_space=pltpu.VMEM)
SMEM = pl.BlockSpec(memory_space=pltpu.SMEM)


def params(mib):
    return pltpu.CompilerParams(vmem_limit_bytes=mib * 2**20)


def cost(flops, size):
    return pl.CostEstimate(flops=flops, bytes_accessed=size, transcendentals=0)


def shift(axis, size, by):
    return [(i, (i + by) % size) for i in range(size)]


def send(array, axis, size, by):
    return lax.ppermute(array, axis, shift(axis, size, by))


def densify_kernel(me_ref, tiles_ref, mine_ref, theirs_ref):
    def clear(p, carry):
        mine_ref[p] = jnp.zeros((PANEL, T), BF16)
        theirs_ref[p] = jnp.zeros((PANEL, T), BF16)
        return carry

    lax.fori_loop(0, Z * X, clear, 0)
    x, core = me_ref[0], me_ref[1]

    def place(k, carry):
        col = me_ref[4 + SLOTS + k]
        offset = (x - (col >> 1) + X) & (X - 1)
        at = offset * Z + (col >> 3)
        span = pl.ds(pl.multiple_of(me_ref[4 + k] * T, T), T)
        own = (col & 1) == core

        @pl.when(own)
        def _():
            mine_ref[at, span, :] = tiles_ref[k]

        @pl.when(jnp.logical_not(own))
        def _():
            theirs_ref[at, span, :] = tiles_ref[k]

        return carry

    lax.fori_loop(0, me_ref[3], place, 0)


def densify(me, tiles):
    return pl.pallas_call(
        densify_kernel,
        in_specs=[SMEM, VMEM],
        out_specs=[VMEM] * 2,
        out_shape=[jax.ShapeDtypeStruct((Z * X, PANEL, T), BF16)] * 2,
        compiler_params=params(16),
        cost_estimate=cost(0, 12 * 2**20),
        name="densify",
    )(me, tiles)


def forward(halves, sources, before, dtype, rider=None):
    count = len(sources)
    places = [(half, n) for half, n, _ in sources]
    extra = [array for array in (before, rider) if array is not None]

    def kernel(*refs):
        out_ref, total = refs[-2:]
        for i, (half, n) in enumerate(places):
            panel = jnp.concatenate([refs[half][n * Z + z] for z in range(Z)], axis=1)
            part = jnp.dot(panel, refs[2 + i][...].reshape(Z * T, T), preferred_element_type=F32)
            if i:
                part += total[...]
            elif before is not None:
                part += refs[2 + count][...]
            if i < count - 1:
                total[...] = part
            else:
                out_ref[:PANEL] = part.astype(dtype)
        if rider is not None:
            out_ref[PANEL:] = refs[3 + count][...]

    return pl.pallas_call(
        kernel,
        in_specs=[VMEM] * (2 + count + len(extra)),
        out_specs=VMEM,
        out_shape=jax.ShapeDtypeStruct((PANEL if rider is None else PANEL + T, T), dtype),
        scratch_shapes=[pltpu.VMEM((PANEL, T), F32)],
        compiler_params=params(16),
        cost_estimate=cost(2 * PANEL * T * T * Z * count, 2**20 * count),
        name="forward",
    )(*halves, *(block for _, _, block in sources), *extra)


def tie(block, token):
    def kernel(block_ref, token_ref, out_ref):
        del block_ref, token_ref, out_ref

    return pl.pallas_call(
        kernel,
        in_specs=[VMEM] * 2,
        out_specs=VMEM,
        out_shape=jax.ShapeDtypeStruct(block.shape, block.dtype),
        input_output_aliases={0: 0},
        compiler_params=params(16),
        name="tie",
    )(block, token)


def split(value):
    high = value.astype(BF16)
    low = (value - high.astype(F32)).astype(BF16)
    return high, low


def pack_bias(ref, start, value):
    high, low = split(value)
    rows = lax.broadcasted_iota(jnp.int32, (16, T), 0)
    packed = jnp.where(rows == 0, high.astype(F32), jnp.where(rows == 1, low.astype(F32), 0.0))
    ref[start:start + 16, :] = packed.astype(BF16)


def middle_kernel(me_ref, p0, p1, p2, p3, weight_ref, bias_ref, own_ref, give_ref, keep_ref, pre, cot, halves):
    core, rep = me_ref[1], me_ref[2]
    for n, source in enumerate((p0, p1, p2, p3)):
        cot[(rep - n + Q) % Q] = source[PANEL:]
    get = lambda ref: ref[:PANEL].astype(F32)
    total = (get(p0) + get(p2)) + (get(p1) + get(p3))
    aggregated = total.astype(BF16)
    preact = jnp.dot(aggregated, weight_ref[...], preferred_element_type=F32) + bias_ref[...]
    pre[...] = preact.reshape(Q, T, T)
    sig = jax.nn.sigmoid(preact)
    cotangent = cot[...].reshape(PANEL, T).astype(F32)
    grad_pre = (cotangent * sig * (1.0 + preact * (1.0 - sig))).astype(BF16)
    own_ref[...] = pre[rep]
    back = lax.dot_general(weight_ref[...], grad_pre, (((1,), (1,)), ((), ())), preferred_element_type=F32)
    for r in range(Q):
        give_ref[r * T:(r + 1) * T] = back[:, r * T:(r + 1) * T].astype(BF16)
    terms = lax.dot_general(aggregated, grad_pre, (((0,), (0,)), ((), ())), preferred_element_type=F32)
    bias_sum = jnp.sum(grad_pre.astype(F32), axis=0, keepdims=True)
    halves[...] = terms.reshape(C, HALF, T)
    keep_ref[...] = halves[core]
    give_ref[PANEL:PANEL + HALF] = halves[1 - core].astype(BF16)
    pack_bias(give_ref, PANEL + HALF, bias_sum)


def middle(me, partials, weight, bias):
    return pl.pallas_call(
        middle_kernel,
        in_specs=[SMEM] + [VMEM] * 6,
        out_specs=[VMEM] * 3,
        out_shape=[
            jax.ShapeDtypeStruct((T, T), F32),
            jax.ShapeDtypeStruct((PANEL + PAY, T), BF16),
            jax.ShapeDtypeStruct((HALF, T), F32),
        ],
        scratch_shapes=[
            pltpu.VMEM((Q, T, T), F32),
            pltpu.VMEM((Q, T, T), BF16),
            pltpu.VMEM((C, HALF, T), F32),
        ],
        compiler_params=params(16),
        cost_estimate=cost(6 * PANEL * T * T, 2**20),
        name="middle",
    )(me, *partials, weight, bias)


def bias_of(ref, start):
    pair = ref[start:start + 16, :].astype(F32)
    return pair[0:1] + pair[1:2]


def wide(ref):
    return jnp.concatenate([ref[r * T:(r + 1) * T] for r in range(Q)], axis=1)


def products(back, panels_ref, chunk, z):
    at = chunk * Z + z
    pair = jnp.concatenate([panels_ref[at], panels_ref[at + 1]], axis=1)
    return jnp.dot(back, pair, preferred_element_type=F32)


def backward_own(mine, give):
    def kernel(mine_ref, give_ref, out_ref):
        back = wide(give_ref)

        def step(chunk, carry):
            for z in range(0, Z, 2):
                part = products(back, mine_ref, chunk, z)
                out_ref[chunk, z] = part[:, :T]
                out_ref[chunk, z + 1] = part[:, T:]
            return carry

        lax.fori_loop(0, X, step, 0)

    return pl.pallas_call(
        kernel,
        in_specs=[VMEM] * 2,
        out_specs=VMEM,
        out_shape=jax.ShapeDtypeStruct((X, Z, T, T), F32),
        compiler_params=params(16),
        cost_estimate=cost(2 * PANEL * T * T * Z * X, 2**22),
        name="backward_own",
    )(mine, give)


def backward(begun, other, give, got, keep, chunk, own=None):
    def kernel(begun_ref, other_ref, give_ref, got_ref, keep_ref, *refs):
        if own is None:
            out_ref, = refs
        else:
            own_ref, out_ref, layer_ref = refs
            preact = own_ref[...]
            layer_ref[...] = (preact * jax.nn.sigmoid(preact)).astype(BF16)
        back = wide(got_ref)
        for z in range(0, Z, 2):
            part = products(back, other_ref, chunk, z)
            out_ref[z * T:z * T + T] = (begun_ref[chunk, z] + part[:, :T]).astype(BF16)
            out_ref[z * T + T:z * T + 2 * T] = (begun_ref[chunk, z + 1] + part[:, T:]).astype(BF16)
        terms = keep_ref[...] + got_ref[PANEL:PANEL + HALF].astype(F32)
        out_ref[Z * T:Z * T + HALF] = terms.astype(BF16)
        bias = bias_of(give_ref, PANEL + HALF) + bias_of(got_ref, PANEL + HALF)
        pack_bias(out_ref, Z * T + HALF, bias)

    extra = [] if own is None else [own]
    return pl.pallas_call(
        kernel,
        in_specs=[VMEM] * (5 + len(extra)),
        out_specs=[VMEM] * (1 + len(extra)),
        out_shape=[jax.ShapeDtypeStruct((MSG, T), BF16)] + [jax.ShapeDtypeStruct((T, T), BF16)] * len(extra),
        compiler_params=params(16),
        cost_estimate=cost(2 * PANEL * T * T * Z, 2**21),
        name="backward",
    )(begun, other, give, got, keep, *extra)


def line_sum(s0, s1, s2, s3):
    def kernel(r0, r1, r2, r3, out_ref):
        def add(a, b):
            get = lambda r: r[a:b].astype(F32)
            return (get(r0) + get(r2)) + (get(r1) + get(r3))

        terms = add(Z * T, Z * T + HALF).astype(BF16)
        at = Z * T + HALF
        bias = (bias_of(r0, at) + bias_of(r2, at)) + (bias_of(r1, at) + bias_of(r3, at))
        for z in range(Z):
            out_ref[z, :T] = add(z * T, z * T + T).astype(BF16)
            out_ref[z, T:T + HALF] = terms
            pack_bias(out_ref.at[z], T + HALF, bias)

    return pl.pallas_call(
        kernel,
        in_specs=[VMEM] * 4,
        out_specs=VMEM,
        out_shape=jax.ShapeDtypeStruct((Z, BLK, T), BF16),
        compiler_params=params(16),
        cost_estimate=cost(0, 2**20),
        name="line_sum",
    )(s0, s1, s2, s3)


def finish_terms(received):
    def kernel(in_ref, half_ref):
        total = in_ref[0, T:T + HALF].astype(F32)
        for z in range(1, Z):
            total += in_ref[z, T:T + HALF].astype(F32)
        half_ref[...] = total * SCALE

    return pl.pallas_call(
        kernel,
        in_specs=[VMEM],
        out_specs=VMEM,
        out_shape=jax.ShapeDtypeStruct((HALF, T), F32),
        compiler_params=params(16),
        cost_estimate=cost(0, 2**18),
        name="finish_terms",
    )(received)


def finish_grad(received):
    def kernel(in_ref, grad_ref, bias_ref):
        total = in_ref[0, :T].astype(F32)
        bias = bias_of(in_ref.at[0], T + HALF)
        for z in range(1, Z):
            total += in_ref[z, :T].astype(F32)
            bias += bias_of(in_ref.at[z], T + HALF)
        grad_ref[...] = total.T.astype(BF16)
        bias_ref[...] = bias * SCALE

    return pl.pallas_call(
        kernel,
        in_specs=[VMEM],
        out_specs=[VMEM] * 2,
        out_shape=[
            jax.ShapeDtypeStruct((T, T), BF16),
            jax.ShapeDtypeStruct((1, T), F32),
        ],
        compiler_params=params(16),
        cost_estimate=cost(0, 2**22),
        name="finish_grad",
    )(received)


def body(features, weight, bias_terms, cotangent, tile_values, tile_rows, tile_cols, tile_count):
    x, core, rep = lax.axis_index("x"), lax.axis_index("core"), lax.axis_index("rep")
    place = jnp.stack([x, core, rep, tile_count[0, 0]]).astype(jnp.int32)
    me = jnp.concatenate([place, tile_rows[0, 0], tile_cols[0, 0]])
    spread = jnp.broadcast_to(features, (Z, T, T))
    line = lax.all_to_all(spread, "z", 0, 0, tiled=True)
    halves = densify(me, tile_values[0, 0])
    begun = forward(halves, [(0, 0, line)], None, F32)
    near = [(1, 0, send(line, "core", C, 1))]
    far = []
    for n in range(1, X):
        block = tie(send(line, "x", X, n), halves[0])
        far += [(0, n, block), (1, n, send(block, "core", C, 1))]
    late = [far[3], far[5]]
    begun = forward(halves, near + far[:3] + far[4:5], begun, F32)
    partial = forward(halves, late, begun, BF16, cotangent)

    partials = [partial] + [send(partial, "rep", Q, n) for n in range(1, Q)]
    mine, theirs = halves
    fellow = send(tie(theirs, partial), "core", C, 1)
    own, give, keep = middle(place, partials, weight, bias_terms.reshape(1, T))
    got = send(give, "core", C, 1)

    ahead = backward_own(mine, give)
    sums = {}
    for n in (1, 2, 3):
        total, = backward(ahead, fellow, give, got, keep, n)
        sums[n] = send(total, "x", X, -n)
    sums[0], output = backward(ahead, fellow, give, got, keep, 0, own)
    blocks = line_sum(sums[0], sums[3], sums[2], sums[1])
    received = lax.all_to_all(blocks, "z", 0, 0, tiled=True)
    half = finish_terms(received)
    other = send(half, "core", C, 1)
    weight_grad = jnp.where(core == 0, jnp.concatenate([half, other]), jnp.concatenate([other, half]))
    grad_input, bias_grad = finish_grad(received)
    return output, grad_input, weight_grad, bias_grad.reshape(T)


def solution(mesh):
    fine = Mesh(mesh.devices.reshape(Z, X, C, Q), ALL)
    return jax.shard_map(
        body,
        mesh=fine,
        in_specs=(
            P(ALL, None),
            P(),
            P(),
            P(ALL, None),
            P(ROW, "rep", None, None, None),
            P(ROW, "rep", None),
            P(ROW, "rep", None),
            P(ROW, "rep"),
        ),
        out_specs=(P(ALL, None), P(ALL, None), P(), P()),
        check_vma=False,
    )
```
